32 devices in a mesh: parts: 2 (over x), grid: 8 (over z, y), depth: 2 (over core).
Axes of the slice: x: 2, y: 2, z: 4, core: 2. Of those that a mesh axis runs over, the one named last changes fastest.
Arguments:
- gate_input: bfloat16 [1024, 32768], P(('parts', 'depth'), 'grid'), parts along dimension 0, may hold values from -6 to 6
- up_input: bfloat16 [1024, 32768], P(('parts', 'depth'), 'grid'), parts along dimension 0, may hold values from -6 to 6
- code_values: bfloat16 [32768, 8192], P('grid', 'depth'), may hold values from -6 to 6, as said below
- exponents: int32 [1024, 8192], P('grid', 'depth'), may hold values from -10 to -7
- cotangent: bfloat16 [1024, 8192], P(('parts', 'depth'), 'grid'), parts along dimension 0, may hold values from -1.5 to 1.5
Outputs:
- output_rows: bfloat16 [1024, 8192], P(('parts', 'depth'), 'grid'), parts along dimension 0
- grad_gate: bfloat16 [1024, 32768], P(('parts', 'depth'), 'grid'), parts along dimension 0
- grad_up: bfloat16 [1024, 32768], P(('parts', 'depth'), 'grid'), parts along dimension 0
- grad_weight: bfloat16 [65536, 8192], P(('parts', 'grid'), 'depth'), parts along dimension 0
The draws below stay inside these ranges and needn't reach their ends.
There are 2 independent parts, one for each index of `parts`. The reference program is written for one: setup_inputs(seed, part) draws one part's arguments, and reference() takes and returns one part's arrays. A program takes and returns all parts, laid end to end along the dimension named above; an argument that names none is the same for every part. Nothing has to cross between parts.
Inputs may be any that keep to these rules, and one draw needn't show every extreme that they name: `code_values`: every entry is one of the E2M1 values 0, +-0.5, +-1, +-1.5, +-2, +-3, +-4, +-6.
All inputs are finite; a program needn't handle non-finite values.
Results may differ from the reference program's by a relative error of at most 0.0049.
Values may be sent and summed in bfloat16 or wider, within the bound.
No kernel may reach another device: no remote copies, remote signals or barrier semaphores. Data moves between devices by JAX's collectives and lax.ppermute only.
A program may use at most 448 MiB of HBM per device.

```python
import jax
import jax.numpy as jnp

D = 8192
FFW = 32768
BLOCK = 32
TOKENS = 512


def draw_code_values(key, part):
    table = jnp.array([0.0, 0.5, 1.0, 1.5, 2.0, 3.0, 4.0, 6.0, 0.0, -0.5, -1.0, -1.5, -2.0, -3.0, -4.0, -6.0], jnp.float32)
    codes = jax.random.randint(jax.random.fold_in(key, 11), (FFW, D), 0, 16)
    return jnp.take(table, codes).astype(jnp.bfloat16)


def set_ends(values, rng, least, largest):
    spot = [jax.random.randint(jax.random.fold_in(rng, axis), (), 0, length) for axis, length in enumerate(values.shape)]
    widest = values.shape.index(max(values.shape))
    beside = spot[:widest] + [(spot[widest] + 1) % values.shape[widest]] + spot[widest + 1:]
    return values.at[tuple(spot)].set(least).at[tuple(beside)].set(largest)


def steps_of(rng, dims, cuts, least, largest):
    def one(dim, parts):
        heights = jax.random.uniform(jax.random.fold_in(jax.random.fold_in(rng, 6), dim), (parts,), jnp.float32, least / len(cuts), largest / len(cuts))
        return jnp.repeat(jnp.exp(heights), dims[dim] // parts).reshape((-1,) + (1,) * (len(dims) - dim - 1))

    gain = one(*cuts[0])
    for cut in cuts[1:]:
        gain = gain * one(*cut)
    return gain


def scatter_about(key, extent, deviation, bound, shards=(), kind=jnp.bfloat16):
    result = deviation * jax.random.normal(key, extent, jnp.float32)
    if shards:
        result = result * steps_of(key, extent, shards, -0.22, 0.18)
    return jnp.clip(result, -bound, bound).astype(kind)


def setup_inputs(seed: int = 0, part: int = 0) -> dict:
    splits = jax.random.split(jax.random.key(seed), 6)
    part_keys = jax.random.split(jax.random.fold_in(splits[5], part), 6)
    gate_input = scatter_about(part_keys[0], (TOKENS, FFW), 1.0, 6.0, ((0, 2), (1, 8)))
    up_input = scatter_about(part_keys[1], (TOKENS, FFW), 1.0, 6.0, ((0, 2), (1, 8)))
    code_values = draw_code_values(jax.random.fold_in(splits[5], 71), part)
    exponents = set_ends(jax.random.randint(splits[3], (FFW // BLOCK, D), -10, -6), jax.random.fold_in(splits[3], 1), -10, (-6) - 1).astype(jnp.int32)
    cotangent = scatter_about(part_keys[4], (TOKENS, D), 0.25, 1.5, ((0, 2), (1, 8)))
    return {"gate_input": gate_input, "up_input": up_input, "code_values": code_values, "exponents": exponents, "cotangent": cotangent}


def dequantize(code_values, exponents):
    scaled = jnp.exp2(exponents.astype(jnp.float32))
    blocks = code_values.astype(jnp.float32).reshape(FFW // BLOCK, BLOCK, D) * scaled[:, None, :]
    return blocks.reshape(FFW, D).astype(jnp.bfloat16)


def reference(gate_input, up_input, code_values, exponents, cotangent):
    weight = dequantize(code_values, exponents)
    gate_float = gate_input.astype(jnp.float32)
    up_float = up_input.astype(jnp.float32)
    sigmoid_gate = jax.nn.sigmoid(gate_float)
    activated = gate_float * sigmoid_gate
    hidden = (activated * up_float).astype(jnp.bfloat16)
    output_rows = jnp.dot(hidden, weight, preferred_element_type=jnp.float32).astype(jnp.bfloat16)
    grad_hidden = jnp.dot(cotangent, weight.T, preferred_element_type=jnp.float32)
    slope = sigmoid_gate * (1.0 + gate_float * (1.0 - sigmoid_gate))
    grad_gate = (grad_hidden * up_float * slope).astype(jnp.bfloat16)
    grad_up = (grad_hidden * activated).astype(jnp.bfloat16)
    grad_weight = jnp.dot(hidden.T, cotangent, preferred_element_type=jnp.float32).astype(jnp.bfloat16)
    return (output_rows, grad_gate, grad_up, grad_weight)
```

```python
import jax
import jax.numpy as jnp
from jax import lax
from jax.experimental import pallas as pl
from jax.experimental.pallas import tpu as pltpu
from jax.sharding import PartitionSpec as P

F32 = jnp.float32
BF16 = jnp.bfloat16
VMEM_BYTES = 56 * 1024 * 1024


def tile_of(size, wanted):
    return min(size, wanted)


def dequantize(codes, scale):
    rows, columns = codes.shape
    blocks = codes.reshape(rows // 32, 32, columns) * scale.reshape(rows // 32, 1, columns)
    return blocks.reshape(rows, columns)


def output_term(hidden, codes, scale):
    tokens, units = hidden.shape
    features = codes.shape[1]
    tile = tile_of(features, 512)
    step = tile_of(units, 1024)

    def body(h_ref, c_ref, s_ref, o_ref):
        total = jnp.zeros((tokens, tile), F32)
        for k in range(0, units, step):
            weight = dequantize(c_ref[k : k + step, :], s_ref[k // 32 : (k + step) // 32, :])
            total += jnp.dot(h_ref[:, k : k + step], weight, preferred_element_type=F32)
        o_ref[...] = total.astype(BF16)

    return pl.pallas_call(
        body,
        grid=(features // tile,),
        in_specs=[
            pl.BlockSpec((tokens, units), lambda j: (0, 0)),
            pl.BlockSpec((units, tile), lambda j: (0, j)),
            pl.BlockSpec((units // 32, tile), lambda j: (0, j)),
        ],
        out_specs=pl.BlockSpec((tokens, tile), lambda j: (0, j)),
        out_shape=jax.ShapeDtypeStruct((tokens, features), BF16),
        compiler_params=pltpu.CompilerParams(vmem_limit_bytes=VMEM_BYTES),
        cost_estimate=pl.CostEstimate(
            flops=2 * tokens * units * features, bytes_accessed=2 * units * features, transcendentals=0
        ),
    )(hidden, codes, scale)


def hidden_gradient(cotangent, codes, scale):
    tokens, features = cotangent.shape
    units = codes.shape[0]
    tile = tile_of(units, 512)
    step = tile_of(features, 1024)

    def body(t_ref, c_ref, s_ref, o_ref):
        total = jnp.zeros((tokens, tile), F32)
        for k in range(0, features, step):
            weight = dequantize(c_ref[:, k : k + step], s_ref[:, k : k + step])
            total += lax.dot_general(
                t_ref[:, k : k + step], weight, (((1,), (1,)), ((), ())), preferred_element_type=F32
            )
        o_ref[...] = total

    return pl.pallas_call(
        body,
        grid=(units // tile,),
        in_specs=[
            pl.BlockSpec((tokens, features), lambda j: (0, 0)),
            pl.BlockSpec((tile, features), lambda j: (j, 0)),
            pl.BlockSpec((tile // 32, features), lambda j: (j, 0)),
        ],
        out_specs=pl.BlockSpec((tokens, tile), lambda j: (0, j)),
        out_shape=jax.ShapeDtypeStruct((tokens, units), F32),
        compiler_params=pltpu.CompilerParams(vmem_limit_bytes=VMEM_BYTES),
        cost_estimate=pl.CostEstimate(
            flops=2 * tokens * units * features, bytes_accessed=2 * units * features, transcendentals=0
        ),
    )(cotangent, codes, scale)


def weight_gradient(hidden, cotangent):
    tokens, units = hidden.shape
    features = cotangent.shape[1]
    tile = tile_of(units, 512)
    step = tile_of(features, 1024)

    def body(h_ref, t_ref, o_ref):
        turned = h_ref[...].T
        for k in range(0, features, step):
            o_ref[:, k : k + step] = jnp.dot(
                turned, t_ref[:, k : k + step], preferred_element_type=F32
            ).astype(BF16)

    return pl.pallas_call(
        body,
        grid=(units // tile,),
        in_specs=[
            pl.BlockSpec((tokens, tile), lambda j: (0, j)),
            pl.BlockSpec((tokens, features), lambda j: (0, 0)),
        ],
        out_specs=pl.BlockSpec((tile, features), lambda j: (j, 0)),
        out_shape=jax.ShapeDtypeStruct((units, features), BF16),
        compiler_params=pltpu.CompilerParams(vmem_limit_bytes=VMEM_BYTES),
        cost_estimate=pl.CostEstimate(
            flops=2 * tokens * units * features, bytes_accessed=2 * units * features, transcendentals=0
        ),
    )(hidden, cotangent)


def shards(n, gate_input, up_input, code_values, exponents, cotangent):
    tokens, part = cotangent.shape
    me = lax.axis_index("depth")
    swap = [(0, 1), (1, 0)]
    half = n // 2

    gathered = lax.all_gather(cotangent, "grid", axis=0, tiled=False)

    gate_float = gate_input.astype(F32)
    up_float = up_input.astype(F32)
    hidden = (gate_float * jax.nn.sigmoid(gate_float) * up_float).astype(BF16)
    scale = jnp.exp2(exponents.astype(F32)).astype(BF16)
    hidden_both = jnp.concatenate([hidden, lax.ppermute(hidden, "depth", swap)], 0)

    partial = output_term(hidden_both, code_values, scale)
    received = lax.ppermute(partial[tokens:], "depth", swap)
    mine = partial[:tokens]
    first = jnp.where(me == 0, mine, received).reshape(tokens, half, part)
    second = jnp.where(me == 0, received, mine).reshape(tokens, half, part)
    pieces = jnp.concatenate([first, second], 1).transpose(1, 0, 2)
    output_rows = lax.psum_scatter(pieces, "grid", scatter_dimension=0, tiled=False)

    keep = lax.dynamic_slice_in_dim(gathered, me * half, half, 0)
    give = lax.dynamic_slice_in_dim(gathered, (1 - me) * half, half, 0)
    got = lax.ppermute(give, "depth", swap)
    cotangent_both = jnp.concatenate([keep, got], 1).transpose(1, 0, 2).reshape(2 * tokens, half * part)

    partial_grad = hidden_gradient(cotangent_both, code_values, scale)
    other_grad = lax.ppermute(partial_grad[tokens:].astype(BF16), "depth", swap)
    grad_weight = weight_gradient(hidden_both, cotangent_both)

    grad_hidden = partial_grad[:tokens] + other_grad.astype(F32)
    gate_float = gate_input.astype(F32)
    up_float = up_input.astype(F32)
    sigmoid_gate = jax.nn.sigmoid(gate_float)
    slope = sigmoid_gate * (1.0 + gate_float * (1.0 - sigmoid_gate))
    grad_gate = (grad_hidden * up_float * slope).astype(BF16)
    grad_up = (grad_hidden * (gate_float * sigmoid_gate)).astype(BF16)
    return (output_rows, grad_gate, grad_up, grad_weight)


def solution(mesh):
    n = mesh.shape["grid"]
    in_specs = (
        P(("parts", "depth"), "grid"),
        P(("parts", "depth"), "grid"),
        P("grid", "depth"),
        P("grid", "depth"),
        P(("parts", "depth"), "grid"),
    )
    out_specs = (
        P(("parts", "depth"), "grid"),
        P(("parts", "depth"), "grid"),
        P(("parts", "depth"), "grid"),
        P(("parts", "grid"), "depth"),
    )

    def step(*arrays):
        return shards(n, *arrays)

    return jax.shard_map(step, mesh=mesh, in_specs=in_specs, out_specs=out_specs, check_vma=False)
```

```python
import functools

import jax
import jax.numpy as jnp
from jax import lax
from jax.experimental import pallas as pl
from jax.experimental.pallas import tpu as pltpu
from jax.sharding import PartitionSpec as P

F32 = jnp.float32
BF16 = jnp.bfloat16
VMEM_BYTES = 30 * 1024 * 1024
SWAP = [(0, 1), (1, 0)]
ANY = pl.BlockSpec(memory_space=pl.ANY)


def params(size=VMEM_BYTES):
    return pltpu.CompilerParams(vmem_limit_bytes=size)


def cost(flops, size):
    return pl.CostEstimate(flops=flops, bytes_accessed=size, transcendentals=0)


def dequantize(codes, exponents):
    rows, columns = codes.shape
    scale = jnp.exp2(exponents.astype(F32)).astype(BF16)
    blocks = codes.reshape(rows // 32, 32, columns) * scale.reshape(rows // 32, 1, columns)
    return blocks.reshape(rows, columns)


def sigmoid(value):
    return 0.5 * jnp.tanh(0.5 * value) + 0.5


def make_hidden(gate, up):
    tokens, units = gate.shape
    tile = min(units, 2048)

    def body(g_ref, u_ref, h_ref, t_ref):
        value = g_ref[...].astype(F32)
        hidden = (value * sigmoid(value) * u_ref[...].astype(F32)).astype(BF16)
        h_ref[...] = hidden
        t_ref[...] = hidden.T

    spec = pl.BlockSpec((tokens, tile), lambda i: (0, i))
    return pl.pallas_call(
        body,
        grid=(units // tile,),
        in_specs=[spec, spec],
        out_specs=[spec, pl.BlockSpec((tile, tokens), lambda i: (i, 0))],
        out_shape=[jax.ShapeDtypeStruct((tokens, units), BF16), jax.ShapeDtypeStruct((units, tokens), BF16)],
        compiler_params=params(60 * 1024 * 1024),
        cost_estimate=cost(10 * tokens * units, 8 * tokens * units),
    )(gate, up)


def finish(gate, up, mine, other, first, so_far, *deps):
    tokens, units = gate.shape
    width = mine.shape[1]
    tile = min(width, 1024)
    base = first // tile

    def body(g_ref, u_ref, m_ref, o_ref, *refs):
        dg_ref, du_ref = refs[-2:]
        value = g_ref[...].astype(F32)
        s = sigmoid(value)
        grad = m_ref[...] + o_ref[...].astype(F32)
        slope = s * (1.0 + value * (1.0 - s))
        dg_ref[...] = (grad * u_ref[...].astype(F32) * slope).astype(BF16)
        du_ref[...] = (grad * (value * s)).astype(BF16)

    there = pl.BlockSpec((tokens, tile), lambda i: (0, base + i))
    here = pl.BlockSpec((tokens, tile), lambda i: (0, i))
    shape = jax.ShapeDtypeStruct((tokens, units), BF16)
    return pl.pallas_call(
        body,
        grid=(width // tile,),
        in_specs=[there, there, here, here] + [ANY] * (len(so_far) + len(deps)),
        out_specs=[there] * 2,
        out_shape=[shape] * 2,
        input_output_aliases={4: 0, 5: 1} if so_far else {},
        compiler_params=params(),
        cost_estimate=cost(20 * tokens * width, 14 * tokens * width),
    )(gate, up, mine, other, *so_far, *deps)


def wait(ref, semaphore):
    pltpu.make_async_copy(ref, ref, semaphore).wait()


def output_terms(places, hidden, hidden_other, codes, exponents, part, deps=(), turn=False):
    tokens, units = hidden.shape
    tile = min(part, 512)
    step = min(units, 1024)
    count = places.shape[0]
    tiles = part // tile
    order = [(j, t) for j in range(count) for t in range(tiles)]
    steps = range(0, units, step)
    outputs = count + (2 if turn else 1)

    def body(p_ref, h_ref, x_ref, c_ref, e_ref, *refs):
        out = refs[len(deps) : len(deps) + outputs]
        held, codes_held, exponents_held, out_held, h_sem, c_sem, e_sem, o_sem, *more = refs[len(deps) + outputs :]

        def columns(i):
            j, t = order[i]
            return pl.ds(pl.multiple_of(p_ref[j] * part + t * tile, tile), tile)

        def fetch(i, rows, semaphore):
            pltpu.make_async_copy(c_ref.at[rows, columns(i)], codes_held.at[i % 2, rows], semaphore).start()

        def fetch_exponents(i):
            pltpu.make_async_copy(e_ref.at[:, columns(i)], exponents_held.at[i % 2], e_sem.at[i % 2]).start()

        def stores(i):
            j, t = order[i]
            lanes = pl.ds(t * tile, tile)
            return [
                pltpu.make_async_copy(out_held.at[i % 2, :tokens], out[j].at[:, lanes], o_sem.at[i % 2, 0]),
                pltpu.make_async_copy(
                    out_held.at[i % 2, tokens:], out[count].at[pl.ds(j * tokens, tokens), lanes], o_sem.at[i % 2, 1]
                ),
            ]

        fetch_exponents(0)
        for n, k in enumerate(steps):
            rows = pl.ds(k, step)
            pltpu.make_async_copy(h_ref.at[:, rows], held.at[:tokens, rows], h_sem.at[n]).start()
            pltpu.make_async_copy(x_ref.at[:, rows], held.at[tokens:, rows], h_sem.at[n]).start()
            fetch(0, rows, c_sem.at[n])
        if len(order) > 1:
            fetch_exponents(1)
            fetch(1, pl.ds(0, units), c_sem.at[len(steps)])
        for i in range(len(order)):
            wait(exponents_held.at[i % 2], e_sem.at[i % 2])
            if i:
                wait(codes_held.at[i % 2], c_sem.at[len(steps) + (i + 1) % 2])
            total = None
            for n, k in enumerate(steps):
                rows = pl.ds(k, step)
                if i == 0:
                    wait(held.at[:, rows], h_sem.at[n])
                    wait(codes_held.at[0, rows], c_sem.at[n])
                weight = dequantize(codes_held[i % 2, rows], exponents_held[i % 2, k // 32 : (k + step) // 32, :])
                term = jnp.dot(held[:, rows], weight, preferred_element_type=F32)
                total = term if total is None else total + term
                if turn and i == 0:
                    turned_held, t_sem = more
                    turned_held[rows] = held[tokens:, rows].T
                    pltpu.make_async_copy(turned_held.at[rows], out[count + 1].at[rows], t_sem.at[n]).start()
            if i >= 2:
                for copy in stores(i - 2):
                    copy.wait()
            out_held[i % 2] = total.astype(BF16)
            for copy in stores(i):
                copy.start()
            if i + 2 < len(order):
                fetch_exponents(i + 2)
                fetch(i + 2, pl.ds(0, units), c_sem.at[len(steps) + (i + 1) % 2])
        for i in range(max(0, len(order) - 2), len(order)):
            for copy in stores(i):
                copy.wait()
        if turn:
            turned_held, t_sem = more
            for n, k in enumerate(steps):
                wait(turned_held.at[pl.ds(k, step)], t_sem.at[n])

    out = pl.pallas_call(
        body,
        in_specs=[pl.BlockSpec(memory_space=pltpu.SMEM)] + [ANY] * (4 + len(deps)),
        out_specs=[ANY] * outputs,
        out_shape=[jax.ShapeDtypeStruct((tokens, part), BF16)] * count
        + [jax.ShapeDtypeStruct((count * tokens, part), BF16)]
        + ([jax.ShapeDtypeStruct((units, tokens), BF16)] if turn else []),
        scratch_shapes=[
            pltpu.VMEM((2 * tokens, units), BF16),
            pltpu.VMEM((2, units, tile), BF16),
            pltpu.VMEM((2, units // 32, tile), jnp.int32),
            pltpu.VMEM((2, 2 * tokens, tile), BF16),
            pltpu.SemaphoreType.DMA((len(steps),)),
            pltpu.SemaphoreType.DMA((len(steps) + 2,)),
            pltpu.SemaphoreType.DMA((2,)),
            pltpu.SemaphoreType.DMA((2, 2)),
        ]
        + ([pltpu.VMEM((units, tokens), BF16), pltpu.SemaphoreType.DMA((len(steps),))] if turn else []),
        compiler_params=params(),
        cost_estimate=cost(4 * tokens * units * part * count, 2 * units * part * count),
    )(places, hidden, hidden_other, codes, exponents, *deps)
    return out[:count], *out[count:]


class Slots:
    def __init__(self, blocks):
        self.blocks = blocks
        self.arrays = [piece[0] for block in blocks for rows in block for piece in rows]
        self.tokens = sum(piece[2] for piece in blocks[0][2])
        self.part = blocks[0][2][0][0].shape[1]

    def scratch(self):
        return [
            pltpu.VMEM((len(self.blocks), 2 * self.tokens, self.part), BF16),
            pltpu.SemaphoreType.DMA((len(self.blocks),)),
        ]

    def load(self, j, flags, refs, held, semaphores):
        before = sum(len(rows) for block in self.blocks[:j] for rows in block)
        refs = iter(refs[before:])
        for wanted, rows in zip((1, 0, None), self.blocks[j]):
            copies, row = [], self.tokens if wanted is None else 0
            for _, first, size in rows:
                copies.append(
                    pltpu.make_async_copy(
                        next(refs).at[pl.ds(first, size)], held.at[j, pl.ds(row, size)], semaphores.at[j]
                    )
                )
                row += size

            def start(copies=copies):
                for copy in copies:
                    copy.start()

            if wanted is None:
                start()
            else:
                pl.when(flags[j] == wanted)(start)


def hidden_gradient(places, flags, slots, codes, exponents, first, width, deps=()):
    tokens, part, count = slots.tokens, slots.part, len(slots.blocks)
    tile = min(width, 512)
    tiles = width // tile
    given = len(slots.arrays)
    step = min(part, 1024)

    def body(p_ref, f_ref, *refs):
        c_ref, e_ref = refs[given : given + 2]
        m_ref, o_ref, held, t_sem, codes_held, exponents_held, m_held, o_held, c_sem, e_sem, o_sem = refs[
            given + 2 + len(deps) :
        ]

        def columns(j):
            return pl.ds(pl.multiple_of(p_ref[j] * part, part), part)

        def fetch(i, j):
            rows = pl.ds(first + i * tile, tile)
            pltpu.make_async_copy(c_ref.at[rows, columns(j)], codes_held.at[i % 2, j], c_sem.at[i % 2, j]).start()

        def stores(i):
            lanes = pl.ds(i * tile, tile)
            return [
                pltpu.make_async_copy(m_held.at[i % 2], m_ref.at[:, lanes], o_sem.at[i % 2, 0]),
                pltpu.make_async_copy(o_held.at[i % 2], o_ref.at[:, lanes], o_sem.at[i % 2, 1]),
            ]

        for j in range(count):
            slots.load(j, f_ref, refs[:given], held, t_sem)
            fetch(0, j)
            rows = pl.ds(first // 32, width // 32)
            pltpu.make_async_copy(e_ref.at[rows, columns(j)], exponents_held.at[j], e_sem.at[j]).start()
        if tiles > 1:
            for j in range(count):
                fetch(1, j)
        for i in range(tiles):
            if i:
                for j in range(count):
                    wait(codes_held.at[i % 2, j], c_sem.at[i % 2, j])
            total = None
            for j in range(count):
                if i == 0:
                    wait(held.at[j], t_sem.at[j])
                    wait(codes_held.at[0, j], c_sem.at[0, j])
                    wait(exponents_held.at[j], e_sem.at[j])
                for k in range(0, part, step):
                    lanes = pl.ds(k, step)
                    weight = dequantize(
                        codes_held[i % 2, j, :, lanes],
                        exponents_held[j, i * tile // 32 : (i + 1) * tile // 32, lanes],
                    )
                    term = lax.dot_general(
                        held[j, :, lanes], weight, (((1,), (1,)), ((), ())), preferred_element_type=F32
                    )
                    total = term if total is None else total + term
            if i >= 2:
                for copy in stores(i - 2):
                    copy.wait()
            m_held[i % 2] = total[:tokens]
            o_held[i % 2] = total[tokens:].astype(BF16)
            for copy in stores(i):
                copy.start()
            if i + 2 < tiles:
                for j in range(count):
                    fetch(i + 2, j)
        for i in range(max(0, tiles - 2), tiles):
            for copy in stores(i):
                copy.wait()

    smem = pl.BlockSpec(memory_space=pltpu.SMEM)
    return pl.pallas_call(
        body,
        in_specs=[smem, smem] + [ANY] * (given + 2 + len(deps)),
        out_specs=[ANY] * 2,
        out_shape=[jax.ShapeDtypeStruct((tokens, width), F32), jax.ShapeDtypeStruct((tokens, width), BF16)],
        scratch_shapes=slots.scratch()
        + [
            pltpu.VMEM((2, count, tile, part), BF16),
            pltpu.VMEM((count, width // 32, part), jnp.int32),
            pltpu.VMEM((2, tokens, tile), F32),
            pltpu.VMEM((2, tokens, tile), BF16),
            pltpu.SemaphoreType.DMA((2, count)),
            pltpu.SemaphoreType.DMA((count,)),
            pltpu.SemaphoreType.DMA((2, 2)),
        ],
        compiler_params=params(),
        cost_estimate=cost(4 * tokens * width * part * count, 2 * width * part * count),
    )(places, flags, *slots.arrays, codes, exponents, *deps)


def weight_gradient(places, flags, slots, turned, turned_other, so_far, features, deps=()):
    part, count = slots.part, len(slots.blocks)
    units, tokens = turned.shape
    tile = min(units, 512)
    tiles = units // tile
    given = len(slots.arrays)
    step = min(part, 1024)
    ahead = min(4, tiles)
    behind = min(4, tiles)

    def body(p_ref, f_ref, *refs):
        h_ref, x_ref = refs[given : given + 2]
        w_ref, held, t_sem, turned_held, out_held, h_sem, o_sem = refs[-7:]

        def fetch(i):
            rows = pl.ds(i * tile, tile)
            slot = i % ahead
            pltpu.make_async_copy(h_ref.at[rows], turned_held.at[slot, :, :tokens], h_sem.at[slot]).start()
            pltpu.make_async_copy(x_ref.at[rows], turned_held.at[slot, :, tokens:], h_sem.at[slot]).start()

        def store(i, j):
            columns = pl.ds(pl.multiple_of(p_ref[j] * part, part), part)
            return pltpu.make_async_copy(
                out_held.at[i % behind, j], w_ref.at[pl.ds(i * tile, tile), columns], o_sem.at[i % behind, j]
            )

        fetch(0)
        for j in range(count):
            slots.load(j, f_ref, refs[:given], held, t_sem)
        for i in range(1, ahead):
            fetch(i)
        for i in range(tiles):
            wait(turned_held.at[i % ahead], h_sem.at[i % ahead])
            left = turned_held[i % ahead]
            for j in range(count):
                if i == 0:
                    wait(held.at[j], t_sem.at[j])
                if i >= behind:
                    store(i - behind, j).wait()
                for k in range(0, part, step):
                    lanes = pl.ds(k, step)
                    out_held[i % behind, j, :, lanes] = jnp.dot(
                        left, held[j, :, lanes], preferred_element_type=F32
                    ).astype(BF16)
                store(i, j).start()
            if i + ahead < tiles:
                fetch(i + ahead)
        for i in range(tiles - behind, tiles):
            for j in range(count):
                store(i, j).wait()

    smem = pl.BlockSpec(memory_space=pltpu.SMEM)
    extra = [] if so_far is None else [so_far]
    return pl.pallas_call(
        body,
        in_specs=[smem, smem] + [ANY] * (given + 2 + len(extra) + len(deps)),
        out_specs=ANY,
        out_shape=jax.ShapeDtypeStruct((units, features), BF16),
        input_output_aliases={4 + given: 0} if extra else {},
        scratch_shapes=slots.scratch()
        + [
            pltpu.VMEM((ahead, tile, 2 * tokens), BF16),
            pltpu.VMEM((behind, count, tile, part), BF16),
            pltpu.SemaphoreType.DMA((ahead,)),
            pltpu.SemaphoreType.DMA((behind, count)),
        ],
        compiler_params=params(),
        cost_estimate=cost(4 * tokens * units * part * count, 2 * units * part * count),
    )(places, flags, *slots.arrays, turned, turned_other, *extra, *deps)


def tie(values, *deps):
    count = len(values)

    def body(*refs):
        pass

    return pl.pallas_call(
        body,
        in_specs=[ANY] * (count + len(deps)),
        out_specs=[ANY] * count,
        out_shape=[jax.ShapeDtypeStruct(v.shape, v.dtype) for v in values],
        input_output_aliases={i: i for i in range(count)},
        compiler_params=params(),
    )(*values, *deps)


def choose(flags, pairs, values, deps):
    arrays = [piece for pair in pairs for block in pair for piece in block]
    tokens, part = sum(p.shape[0] for p in pairs[0][0]), pairs[0][0][0].shape[1]
    count, kept = len(arrays), len(values)

    def body(f_ref, *refs):
        o_ref, semaphore = refs[-2 - kept], refs[-1]
        given = iter(refs[:count])
        for j, pair in enumerate(pairs):
            for wanted, block in zip((1, 0), pair):
                copies, row = [], j * tokens
                for piece in block:
                    size = piece.shape[0]
                    copies.append(pltpu.make_async_copy(next(given), o_ref.at[pl.ds(row, size)], semaphore))
                    row += size

                @pl.when(f_ref[j] == wanted)
                def _(copies=copies):
                    for copy in copies:
                        copy.start()

        pltpu.make_async_copy(o_ref, o_ref, semaphore).wait()

    return pl.pallas_call(
        body,
        in_specs=[pl.BlockSpec(memory_space=pltpu.SMEM)] + [ANY] * (count + kept + len(deps)),
        out_specs=[ANY] * (1 + kept),
        out_shape=[jax.ShapeDtypeStruct((len(pairs) * tokens, part), BF16)]
        + [jax.ShapeDtypeStruct(v.shape, v.dtype) for v in values],
        input_output_aliases={1 + count + i: 1 + i for i in range(kept)},
        scratch_shapes=[pltpu.SemaphoreType.DMA],
        compiler_params=params(),
    )(flags, *arrays, *values, *deps)


def ring_shards(n, gate_input, up_input, code_values, exponents, cotangent):
    tokens, part = cotangent.shape
    units, features = code_values.shape
    lines = n // 2
    ring = [2 * p for p in range(lines)] + [2 * (n - 1 - p) + 1 for p in range(lines, n)]
    forward = [(ring[p], ring[(p + 1) % n]) for p in range(n)]
    backward = [(b, a) for a, b in forward]
    core = lax.axis_index("depth")
    index = lax.axis_index("grid")
    line = index // 2
    here = jnp.where(index % 2 == 0, line, n - 1 - line)

    def owner(offset):
        p = (here + offset + n) % n
        return jnp.where(p < lines, 2 * p, 2 * (n - 1 - p) + 1)

    def swap(value):
        return lax.ppermute(value, "depth", SWAP)

    def on(value):
        return lax.ppermute(value, "grid", forward)

    def back(value):
        return lax.ppermute(value, "grid", backward)

    pairs = [(4, 0), (3, -1), (-3, 1), (2, -2)]
    mine = [owner(a) // lines == core for a, _ in pairs]
    place = [jnp.where(m, owner(a), owner(b)) % lines for (a, b), m in zip(pairs, mine)]

    def places(*group):
        return jnp.stack([place[j] for j in group]).astype(jnp.int32)

    def flags(*group):
        return jnp.stack([mine[j] for j in group]).astype(jnp.int32)

    half = tokens // 2
    block, got, term = {0: [cotangent]}, {}, {}

    def pieces(rows):
        return [(piece, 0, piece.shape[0]) for piece in rows]

    def terms(*group, deps=()):
        own, others, *turned = output_terms(
            places(*group), hidden, hidden_other, code_values, exponents, part, deps, group == (0,)
        )
        return own, swap(others), *turned

    def keep_terms(group, own, others):
        for i, j in enumerate(group):
            a, b = pairs[j]
            other = others[i * tokens : (i + 1) * tokens]
            term[a] = jnp.where(mine[j], own[i], other)
            term[b] = jnp.where(mine[j], other, own[i])

    def slots(*group):
        return Slots([[pieces(block[a]), pieces(block[b]), got[j]] for j in group for a, b in (pairs[j],)])

    def gradient(so_far, group, deps=()):
        return weight_gradient(
            places(*group), flags(*group), slots(*group), turned, turned_other, so_far, features, deps
        )

    def add(value, other):
        return (value.astype(F32) + other.astype(F32)).astype(BF16)

    def exchange(group, values, *deps):
        chosen = [(block[pairs[j][1]], block[pairs[j][0]]) for j in group]
        given, *values = choose(flags(*group), chosen, values, deps)
        found = swap(given)
        for i, j in enumerate(group):
            got[j] = [(found, i * tokens, tokens)]
        return values

    block[-1], block[1] = [on(cotangent)], [back(cotangent)]
    hidden, turned = make_hidden(gate_input, up_input)
    hidden_other = swap(hidden)

    own_a, others_a, turned_other = terms(0)
    first, second = tie([block[-1][0], block[1][0]], own_a[0])
    block[-1], block[1] = [first], [second]
    block[-2], block[2] = [on(first)], [back(second)]

    own_b, others_b = terms(1, 2, deps=(first, second))
    first, second = tie([block[-2][0], block[2][0]], own_b[0])
    block[-2], block[2] = [first], [second]
    block[-3], block[3] = [on(first)], [back(second)]
    exchange((3,), [])

    own_c, others_c = terms(3, deps=(first, second))
    (others_a,) = tie([others_a], own_c[0])
    keep_terms((0,), own_a, others_a)
    up, down = on(term[4][:half]), back(term[4][half:])
    grad_weight = gradient(None, (3,), (own_c[0], term[4]))

    first, second, up, down = tie([block[-3][0], block[3][0], up, down], grad_weight)
    block[-3], block[3] = [first], [second]
    block[4] = [on(first[:half]), back(second[half:])]
    exchange((1, 2), [])
    keep_terms((1, 2), own_b, others_b)
    zero = jnp.zeros((half, part), BF16)
    up, down = add(jnp.concatenate([up, zero], 0), term[3]), add(jnp.concatenate([zero, down], 0), term[-3])
    deps = (up, down)
    up, down = on(up), back(down)
    grad_weight = gradient(grad_weight, (1, 2), deps)

    *block[4], up, down = tie([*block[4], up, down], grad_weight)
    exchange((0,), [])
    keep_terms((3,), own_c, others_c)
    up, down = add(up, term[2]), add(down, term[-2])
    deps = (up, down)
    up, down = on(up), back(down)

    everything = slots(0, 1, 2, 3)
    width = units // 2

    def gradients(start, deps):
        own, give = hidden_gradient(
            places(0, 1, 2, 3), flags(0, 1, 2, 3), everything, code_values, exponents, start, width, deps
        )
        return own, give, swap(give)

    own_left, give, other_left = gradients(0, deps)
    up, down = tie([up, down], give)
    up, down = add(up, term[1]), add(down, term[-1])
    deps = (up, down)
    up, down = on(up), back(down)
    own_right, give, other_right = gradients(width, deps)
    up, down = tie([up, down], give)
    output_rows = (up.astype(F32) + down.astype(F32) + term[0].astype(F32)).astype(BF16)
    grad_weight = gradient(grad_weight, (0,), (output_rows,))
    done = finish(gate_input, up_input, own_left, other_left, 0, [], grad_weight)
    done = finish(gate_input, up_input, own_right, other_right, width, done)
    return output_rows, done[0], done[1], grad_weight


def any_shards(n, gate_input, up_input, code_values, exponents, cotangent):
    tokens, part = cotangent.shape
    units, features = code_values.shape
    core = lax.axis_index("depth")
    half = n // 2
    gathered = lax.all_gather(cotangent, "grid", axis=0, tiled=False)
    hidden, turned = make_hidden(gate_input, up_input)
    hidden_other = lax.ppermute(hidden, "depth", SWAP)
    place, flag = jnp.zeros((1,), jnp.int32), jnp.ones((1,), jnp.int32)

    (own,), other, turned_other = output_terms(
        place, hidden, hidden_other, code_values, exponents, features, turn=True
    )
    got = lax.ppermute(other, "depth", SWAP)
    first = jnp.where(core == 0, own, got).reshape(tokens, half, part)
    second = jnp.where(core == 0, got, own).reshape(tokens, half, part)
    pieces = jnp.concatenate([first, second], 1).transpose(1, 0, 2)
    output_rows = lax.psum_scatter(pieces, "grid", scatter_dimension=0, tiled=False)

    keep = lax.dynamic_slice_in_dim(gathered, core * half, half, 0)
    give = lax.dynamic_slice_in_dim(gathered, (1 - core) * half, half, 0)
    both = [keep, lax.ppermute(give, "depth", SWAP)]
    own, other = ([(v.transpose(1, 0, 2).reshape(tokens, features), 0, tokens)] for v in both)
    slots = Slots([[own, own, other]])
    grad_mine, grad_give = hidden_gradient(place, flag, slots, code_values, exponents, 0, units)
    grad_other = lax.ppermute(grad_give, "depth", SWAP)
    grad_weight = weight_gradient(place, flag, slots, turned, turned_other, None, features)
    grad_gate, grad_up = finish(gate_input, up_input, grad_mine, grad_other, 0, [])
    return output_rows, grad_gate, grad_up, grad_weight


def solution(mesh):
    n = mesh.shape["grid"]
    in_specs = (
        P(("parts", "depth"), "grid"),
        P(("parts", "depth"), "grid"),
        P("grid", "depth"),
        P("grid", "depth"),
        P(("parts", "depth"), "grid"),
    )
    out_specs = (
        P(("parts", "depth"), "grid"),
        P(("parts", "depth"), "grid"),
        P(("parts", "depth"), "grid"),
        P(("parts", "grid"), "depth"),
    )
    step = functools.partial(ring_shards if n == 8 else any_shards, n)
    return jax.shard_map(step, mesh=mesh, in_specs=in_specs, out_specs=out_specs, check_vma=False)
```

```python
import functools

import jax
import jax.numpy as jnp
from jax import lax
from jax.experimental import pallas as pl
from jax.experimental.pallas import tpu as pltpu
from jax.sharding import PartitionSpec as P

F32 = jnp.float32
BF16 = jnp.bfloat16
VMEM_BYTES = 30 * 1024 * 1024
SWAP = [(0, 1), (1, 0)]
ANY = pl.BlockSpec(memory_space=pl.ANY)


def params(size=VMEM_BYTES):
    return pltpu.CompilerParams(vmem_limit_bytes=size)


def cost(flops, size):
    return pl.CostEstimate(flops=flops, bytes_accessed=size, transcendentals=0)


def dequantize(codes, exponents):
    rows, columns = codes.shape
    scale = jnp.exp2(exponents.astype(F32)).astype(BF16)
    blocks = codes.reshape(rows // 32, 32, columns) * scale.reshape(rows // 32, 1, columns)
    return blocks.reshape(rows, columns)


def sigmoid(value):
    return 0.5 * jnp.tanh(0.5 * value) + 0.5


def make_hidden(gate, up):
    tokens, units = gate.shape
    tile = min(units, 1024)
    tiles = units // tile

    def body(g_ref, u_ref, h_ref, gate_held, up_held, out_held, in_sem, out_sem):
        def columns(i):
            return pl.ds(i * tile, tile)

        def store(i):
            return pltpu.make_async_copy(out_held.at[i], h_ref.at[:, columns(i)], out_sem.at[i])

        for i in range(tiles):
            pltpu.make_async_copy(g_ref.at[:, columns(i)], gate_held.at[i], in_sem.at[i, 0]).start()
            pltpu.make_async_copy(u_ref.at[:, columns(i)], up_held.at[i], in_sem.at[i, 1]).start()
        for i in range(tiles):
            wait(gate_held.at[i], in_sem.at[i, 0])
            wait(up_held.at[i], in_sem.at[i, 1])
            value = gate_held[i].astype(F32)
            out_held[i] = (value * sigmoid(value) * up_held[i].astype(F32)).astype(BF16)
            store(i).start()
        for i in range(tiles):
            store(i).wait()

    held = pltpu.VMEM((tiles, tokens, tile), BF16)
    return pl.pallas_call(
        body,
        in_specs=[ANY] * 2,
        out_specs=ANY,
        out_shape=jax.ShapeDtypeStruct((tokens, units), BF16),
        scratch_shapes=[held, held, held, pltpu.SemaphoreType.DMA((tiles, 2)), pltpu.SemaphoreType.DMA((tiles,))],
        compiler_params=params(60 * 1024 * 1024),
        cost_estimate=cost(10 * tokens * units, 6 * tokens * units),
    )(gate, up)


def finish(gate, up, mine, other, first, so_far, *deps):
    tokens, units = gate.shape
    width = mine.shape[1]
    tile = min(width, 1024)
    base = first // tile

    def body(g_ref, u_ref, m_ref, o_ref, *refs):
        dg_ref, du_ref = refs[-2:]
        value = g_ref[...].astype(F32)
        s = sigmoid(value)
        grad = m_ref[...] + o_ref[...].astype(F32)
        slope = s * (1.0 + value * (1.0 - s))
        dg_ref[...] = (grad * u_ref[...].astype(F32) * slope).astype(BF16)
        du_ref[...] = (grad * (value * s)).astype(BF16)

    there = pl.BlockSpec((tokens, tile), lambda i: (0, base + i))
    here = pl.BlockSpec((tokens, tile), lambda i: (0, i))
    shape = jax.ShapeDtypeStruct((tokens, units), BF16)
    return pl.pallas_call(
        body,
        grid=(width // tile,),
        in_specs=[there, there, here, here] + [ANY] * (len(so_far) + len(deps)),
        out_specs=[there] * 2,
        out_shape=[shape] * 2,
        input_output_aliases={4: 0, 5: 1} if so_far else {},
        compiler_params=params(),
        cost_estimate=cost(20000 * tokens * width, 1000 * tokens * width),
    )(gate, up, mine, other, *so_far, *deps)


def wait(ref, semaphore):
    pltpu.make_async_copy(ref, ref, semaphore).wait()


def output_terms(places, hidden, hidden_other, codes, exponents, part, deps=(), turn=False):
    tokens, units = hidden.shape
    tile = min(part, 512)
    step = min(units, 1024)
    count = places.shape[0]
    tiles = part // tile
    order = [(j, t) for j in range(count) for t in range(tiles)]
    steps = range(0, units, step)
    outputs = count + (2 if turn else 1)

    def body(p_ref, h_ref, x_ref, c_ref, e_ref, *refs):
        out = refs[len(deps) : len(deps) + outputs]
        held, codes_held, exponents_held, out_held, h_sem, c_sem, e_sem, o_sem, *more = refs[len(deps) + outputs :]

        def columns(i):
            j, t = order[i]
            return pl.ds(pl.multiple_of(p_ref[j] * part + t * tile, tile), tile)

        def fetch(i, rows, semaphore):
            pltpu.make_async_copy(c_ref.at[rows, columns(i)], codes_held.at[i % 2, rows], semaphore).start()

        def fetch_exponents(i):
            pltpu.make_async_copy(e_ref.at[:, columns(i)], exponents_held.at[i % 2], e_sem.at[i % 2]).start()

        def stores(i):
            j, t = order[i]
            lanes = pl.ds(t * tile, tile)
            return [
                pltpu.make_async_copy(out_held.at[i % 2, :tokens], out[j].at[:, lanes], o_sem.at[i % 2, 0]),
                pltpu.make_async_copy(
                    out_held.at[i % 2, tokens:], out[count].at[pl.ds(j * tokens, tokens), lanes], o_sem.at[i % 2, 1]
                ),
            ]

        fetch_exponents(0)
        for n, k in enumerate(steps):
            rows = pl.ds(k, step)
            pltpu.make_async_copy(h_ref.at[:, rows], held.at[:tokens, rows], h_sem.at[n]).start()
            pltpu.make_async_copy(x_ref.at[:, rows], held.at[tokens:, rows], h_sem.at[n]).start()
            fetch(0, rows, c_sem.at[n])
        if len(order) > 1:
            fetch_exponents(1)
            fetch(1, pl.ds(0, units), c_sem.at[len(steps)])
        for i in range(len(order)):
            wait(exponents_held.at[i % 2], e_sem.at[i % 2])
            if i:
                wait(codes_held.at[i % 2], c_sem.at[len(steps) + (i + 1) % 2])
            total = None
            for n, k in enumerate(steps):
                rows = pl.ds(k, step)
                if i == 0:
                    wait(held.at[:, rows], h_sem.at[n])
                    wait(codes_held.at[0, rows], c_sem.at[n])
                weight = dequantize(codes_held[i % 2, rows], exponents_held[i % 2, k // 32 : (k + step) // 32, :])
                term = jnp.dot(held[:, rows], weight, preferred_element_type=F32)
                total = term if total is None else total + term
                if turn and i == 0:
                    turned_held, t_sem = more
                    turned_held[rows] = held[:, rows].T
                    pltpu.make_async_copy(turned_held.at[rows], out[count + 1].at[rows], t_sem.at[n]).start()
            if i >= 2:
                for copy in stores(i - 2):
                    copy.wait()
            out_held[i % 2] = total.astype(BF16)
            for copy in stores(i):
                copy.start()
            if i + 2 < len(order):
                fetch_exponents(i + 2)
                fetch(i + 2, pl.ds(0, units), c_sem.at[len(steps) + (i + 1) % 2])
        for i in range(max(0, len(order) - 2), len(order)):
            for copy in stores(i):
                copy.wait()
        if turn:
            turned_held, t_sem = more
            for n, k in enumerate(steps):
                wait(turned_held.at[pl.ds(k, step)], t_sem.at[n])

    out = pl.pallas_call(
        body,
        in_specs=[pl.BlockSpec(memory_space=pltpu.SMEM)] + [ANY] * (4 + len(deps)),
        out_specs=[ANY] * outputs,
        out_shape=[jax.ShapeDtypeStruct((tokens, part), BF16)] * count
        + [jax.ShapeDtypeStruct((count * tokens, part), BF16)]
        + ([jax.ShapeDtypeStruct((units, 2 * tokens), BF16)] if turn else []),
        scratch_shapes=[
            pltpu.VMEM((2 * tokens, units), BF16),
            pltpu.VMEM((2, units, tile), BF16),
            pltpu.VMEM((2, units // 32, tile), jnp.int32),
            pltpu.VMEM((2, 2 * tokens, tile), BF16),
            pltpu.SemaphoreType.DMA((len(steps),)),
            pltpu.SemaphoreType.DMA((len(steps) + 2,)),
            pltpu.SemaphoreType.DMA((2,)),
            pltpu.SemaphoreType.DMA((2, 2)),
        ]
        + ([pltpu.VMEM((units, 2 * tokens), BF16), pltpu.SemaphoreType.DMA((len(steps),))] if turn else []),
        compiler_params=params(),
        cost_estimate=cost(4 * tokens * units * part * count, 2 * units * part * count),
    )(places, hidden, hidden_other, codes, exponents, *deps)
    return out[:count], *out[count:]


class Slots:
    def __init__(self, blocks):
        self.blocks = blocks
        self.arrays = [piece[0] for block in blocks for rows in block for piece in rows]
        self.tokens = sum(piece[2] for piece in blocks[0][2])
        self.part = blocks[0][2][0][0].shape[1]

    def scratch(self):
        return [
            pltpu.VMEM((len(self.blocks), 2 * self.tokens, self.part), BF16),
            pltpu.SemaphoreType.DMA((len(self.blocks),)),
        ]

    def load(self, j, flags, refs, held, semaphores):
        before = sum(len(rows) for block in self.blocks[:j] for rows in block)
        refs = iter(refs[before:])
        for wanted, rows in zip((1, 0, None), self.blocks[j]):
            copies, row = [], self.tokens if wanted is None else 0
            for _, first, size in rows:
                copies.append(
                    pltpu.make_async_copy(
                        next(refs).at[pl.ds(first, size)], held.at[j, pl.ds(row, size)], semaphores.at[j]
                    )
                )
                row += size

            def start(copies=copies):
                for copy in copies:
                    copy.start()

            if wanted is None:
                start()
            else:
                pl.when(flags[j] == wanted)(start)


def run(phases, deps=(), size=VMEM_BYTES):
    smem = pl.BlockSpec(memory_space=pltpu.SMEM)
    ends = []
    aliases = {}
    given, made, held = 0, 0, 0
    for phase in phases:
        for i, o in phase["aliases"].items():
            aliases[given + i] = made + o
        ends.append((given, made, held))
        given += phase["scalars"] + len(phase["inputs"])
        made += len(phase["shapes"])
        held += len(phase["scratch"])
    ends.append((given, made, held))

    def body(*refs):
        inputs, outputs = refs[:given], refs[given + len(deps) : given + len(deps) + made]
        scratch = refs[given + len(deps) + made :]
        steps = []
        for phase, (i, o, h), (i_end, o_end, h_end) in zip(phases, ends, ends[1:]):
            steps.append(phase["body"](*inputs[i:i_end], *outputs[o:o_end], *scratch[h:h_end]))
        for step in steps:
            next(step)
        for step in steps:
            next(step, None)

    out = pl.pallas_call(
        body,
        in_specs=[
            spec for p in phases for spec in [smem] * p["scalars"] + [ANY] * len(p["inputs"])
        ]
        + [ANY] * len(deps),
        out_specs=[ANY] * made,
        out_shape=[shape for p in phases for shape in p["shapes"]],
        input_output_aliases=aliases,
        scratch_shapes=[shape for p in phases for shape in p["scratch"]],
        compiler_params=params(size),
        cost_estimate=cost(sum(p["flops"] for p in phases), sum(p["size"] for p in phases)),
    )(*[value for p in phases for value in p["numbers"] + p["inputs"]], *deps)
    return [out[a[1] : b[1]] for a, b in zip(ends, ends[1:])]


def hidden_gradient(places, flags, slots, codes, exponents, first, width):
    tokens, part, count = slots.tokens, slots.part, len(slots.blocks)
    tile = min(width, 512)
    tiles = width // tile
    given = len(slots.arrays)
    step = min(part, 1024)

    def body(p_ref, f_ref, *refs):
        c_ref, e_ref = refs[given : given + 2]
        m_ref, o_ref, held, t_sem, codes_held, exponents_held, m_held, o_held, c_sem, e_sem, o_sem = refs[given + 2 :]

        def columns(j):
            return pl.ds(pl.multiple_of(p_ref[j] * part, part), part)

        def fetch(i, j):
            rows = pl.ds(first + i * tile, tile)
            pltpu.make_async_copy(c_ref.at[rows, columns(j)], codes_held.at[i % 2, j], c_sem.at[i % 2, j]).start()

        def stores(i):
            lanes = pl.ds(i * tile, tile)
            return [
                pltpu.make_async_copy(m_held.at[i % 2], m_ref.at[:, lanes], o_sem.at[i % 2, 0]),
                pltpu.make_async_copy(o_held.at[i % 2], o_ref.at[:, lanes], o_sem.at[i % 2, 1]),
            ]

        for j in range(count):
            slots.load(j, f_ref, refs[:given], held, t_sem)
            fetch(0, j)
            rows = pl.ds(first // 32, width // 32)
            pltpu.make_async_copy(e_ref.at[rows, columns(j)], exponents_held.at[j], e_sem.at[j]).start()
        if tiles > 1:
            for j in range(count):
                fetch(1, j)
        yield
        for i in range(tiles):
            if i:
                for j in range(count):
                    wait(codes_held.at[i % 2, j], c_sem.at[i % 2, j])
            total = None
            for j in range(count):
                if i == 0:
                    wait(held.at[j], t_sem.at[j])
                    wait(codes_held.at[0, j], c_sem.at[0, j])
                    wait(exponents_held.at[j], e_sem.at[j])
                for k in range(0, part, step):
                    lanes = pl.ds(k, step)
                    weight = dequantize(
                        codes_held[i % 2, j, :, lanes],
                        exponents_held[j, i * tile // 32 : (i + 1) * tile // 32, lanes],
                    )
                    term = lax.dot_general(
                        held[j, :, lanes], weight, (((1,), (1,)), ((), ())), preferred_element_type=F32
                    )
                    total = term if total is None else total + term
            if i >= 2:
                for copy in stores(i - 2):
                    copy.wait()
            m_held[i % 2] = total[:tokens]
            o_held[i % 2] = total[tokens:].astype(BF16)
            for copy in stores(i):
                copy.start()
            if i + 2 < tiles:
                for j in range(count):
                    fetch(i + 2, j)
        for i in range(max(0, tiles - 2), tiles):
            for copy in stores(i):
                copy.wait()

    return dict(
        body=body,
        scalars=2,
        numbers=[places, flags],
        inputs=[*slots.arrays, codes, exponents],
        shapes=[jax.ShapeDtypeStruct((tokens, width), F32), jax.ShapeDtypeStruct((tokens, width), BF16)],
        aliases={},
        scratch=slots.scratch()
        + [
            pltpu.VMEM((2, count, tile, part), BF16),
            pltpu.VMEM((count, width // 32, part), jnp.int32),
            pltpu.VMEM((2, tokens, tile), F32),
            pltpu.VMEM((2, tokens, tile), BF16),
            pltpu.SemaphoreType.DMA((2, count)),
            pltpu.SemaphoreType.DMA((count,)),
            pltpu.SemaphoreType.DMA((2, 2)),
        ],
        flops=4 * tokens * width * part * count,
        size=2 * width * part * count,
    )


def weight_gradient(places, flags, slots, turned, so_far, features):
    part, count = slots.part, len(slots.blocks)
    units, rows_all = turned.shape
    tile = min(units, 512)
    tiles = units // tile
    given = len(slots.arrays)
    step = min(part, 1024)
    ahead = min(4, tiles)
    behind = min(4, tiles)

    def body(p_ref, f_ref, *refs):
        h_ref = refs[given]
        w_ref, held, t_sem, turned_held, out_held, h_sem, o_sem = refs[-7:]

        def fetch(i):
            rows = pl.ds(i * tile, tile)
            slot = i % ahead
            pltpu.make_async_copy(h_ref.at[rows], turned_held.at[slot], h_sem.at[slot]).start()

        def store(i, j):
            columns = pl.ds(pl.multiple_of(p_ref[j] * part, part), part)
            return pltpu.make_async_copy(
                out_held.at[i % behind, j], w_ref.at[pl.ds(i * tile, tile), columns], o_sem.at[i % behind, j]
            )

        fetch(0)
        for j in range(count):
            slots.load(j, f_ref, refs[:given], held, t_sem)
        for i in range(1, ahead):
            fetch(i)
        yield
        for i in range(tiles):
            wait(turned_held.at[i % ahead], h_sem.at[i % ahead])
            left = turned_held[i % ahead]
            if i >= behind:
                for j in range(count):
                    store(i - behind, j).wait()
            for j in range(count):
                if i == 0:
                    wait(held.at[j], t_sem.at[j])
                for k in range(0, part, step):
                    lanes = pl.ds(k, step)
                    out_held[i % behind, j, :, lanes] = jnp.dot(
                        left, held[j, :, lanes], preferred_element_type=F32
                    ).astype(BF16)
                if i == 0:
                    store(i, j).start()
            if i:
                for j in range(count):
                    store(i, j).start()
            if i + ahead < tiles:
                fetch(i + ahead)
        for i in range(tiles - behind, tiles):
            for j in range(count):
                store(i, j).wait()

    extra = [] if so_far is None else [so_far]
    return dict(
        body=body,
        scalars=2,
        numbers=[places, flags],
        inputs=[*slots.arrays, turned, *extra],
        shapes=[jax.ShapeDtypeStruct((units, features), BF16)],
        aliases={3 + given: 0} if extra else {},
        scratch=slots.scratch()
        + [
            pltpu.VMEM((ahead, tile, rows_all), BF16),
            pltpu.VMEM((behind, count, tile, part), BF16),
            pltpu.SemaphoreType.DMA((ahead,)),
            pltpu.SemaphoreType.DMA((behind, count)),
        ],
        flops=2 * rows_all * units * part * count,
        size=2 * units * part * count,
    )


def tie(values, *deps):
    count = len(values)

    def body(*refs):
        pass

    return pl.pallas_call(
        body,
        in_specs=[ANY] * (count + len(deps)),
        out_specs=[ANY] * count,
        out_shape=[jax.ShapeDtypeStruct(v.shape, v.dtype) for v in values],
        input_output_aliases={i: i for i in range(count)},
        compiler_params=params(),
    )(*values, *deps)


def choose(flags, pairs, values, deps):
    arrays = [piece for pair in pairs for block in pair for piece in block]
    tokens, part = sum(p.shape[0] for p in pairs[0][0]), pairs[0][0][0].shape[1]
    count, kept = len(arrays), len(values)

    def body(f_ref, *refs):
        o_ref, semaphore = refs[-2 - kept], refs[-1]
        given = iter(refs[:count])
        for j, pair in enumerate(pairs):
            for wanted, block in zip((1, 0), pair):
                copies, row = [], j * tokens
                for piece in block:
                    size = piece.shape[0]
                    copies.append(pltpu.make_async_copy(next(given), o_ref.at[pl.ds(row, size)], semaphore))
                    row += size

                @pl.when(f_ref[j] == wanted)
                def _(copies=copies):
                    for copy in copies:
                        copy.start()

        pltpu.make_async_copy(o_ref, o_ref, semaphore).wait()

    return pl.pallas_call(
        body,
        in_specs=[pl.BlockSpec(memory_space=pltpu.SMEM)] + [ANY] * (count + kept + len(deps)),
        out_specs=[ANY] * (1 + kept),
        out_shape=[jax.ShapeDtypeStruct((len(pairs) * tokens, part), BF16)]
        + [jax.ShapeDtypeStruct(v.shape, v.dtype) for v in values],
        input_output_aliases={1 + count + i: 1 + i for i in range(kept)},
        scratch_shapes=[pltpu.SemaphoreType.DMA],
        compiler_params=params(),
    )(flags, *arrays, *values, *deps)


def ring_shards(n, gate_input, up_input, code_values, exponents, cotangent):
    tokens, part = cotangent.shape
    units, features = code_values.shape
    lines = n // 2
    ring = [2 * p for p in range(lines)] + [2 * (n - 1 - p) + 1 for p in range(lines, n)]
    forward = [(ring[p], ring[(p + 1) % n]) for p in range(n)]
    backward = [(b, a) for a, b in forward]
    core = lax.axis_index("depth")
    index = lax.axis_index("grid")
    line = index // 2
    here = jnp.where(index % 2 == 0, line, n - 1 - line)

    def owner(offset):
        p = (here + offset + n) % n
        return jnp.where(p < lines, 2 * p, 2 * (n - 1 - p) + 1)

    def swap(value):
        return lax.ppermute(value, "depth", SWAP)

    def on(value):
        return lax.ppermute(value, "grid", forward)

    def back(value):
        return lax.ppermute(value, "grid", backward)

    pairs = [(4, 0), (3, -1), (-3, 1), (2, -2)]
    mine = [owner(a) // lines == core for a, _ in pairs]
    place = [jnp.where(m, owner(a), owner(b)) % lines for (a, b), m in zip(pairs, mine)]

    def places(*group):
        return jnp.stack([place[j] for j in group]).astype(jnp.int32)

    def flags(*group):
        return jnp.stack([mine[j] for j in group]).astype(jnp.int32)

    half = tokens // 2
    block, got, term = {0: [cotangent]}, {}, {}

    def pieces(rows):
        return [(piece, 0, piece.shape[0]) for piece in rows]

    def terms(*group, deps=()):
        own, others, *turned = output_terms(
            places(*group), hidden, hidden_other, code_values, exponents, part, deps, group == (0,)
        )
        return own, swap(others), *turned

    def keep_terms(group, own, others):
        for i, j in enumerate(group):
            a, b = pairs[j]
            other = others[i * tokens : (i + 1) * tokens]
            term[a] = jnp.where(mine[j], own[i], other)
            term[b] = jnp.where(mine[j], other, own[i])

    def slots(*group):
        return Slots([[pieces(block[a]), pieces(block[b]), got[j]] for j in group for a, b in (pairs[j],)])

    def weight_phase(so_far, group):
        return weight_gradient(places(*group), flags(*group), slots(*group), turned, so_far, features)

    def gradient(so_far, group, deps=()):
        (((out,)),) = run([weight_phase(so_far, group)], deps)
        return out

    def add(value, other):
        return (value.astype(F32) + other.astype(F32)).astype(BF16)

    def exchange(group, values, *deps):
        chosen = [(block[pairs[j][1]], block[pairs[j][0]]) for j in group]
        given, *values = choose(flags(*group), chosen, values, deps)
        found = swap(given)
        for i, j in enumerate(group):
            got[j] = [(found, i * tokens, tokens)]
        return values

    block[-1], block[1] = [on(cotangent)], [back(cotangent)]
    hidden = make_hidden(gate_input, up_input)
    hidden_other = swap(hidden)

    own_a, others_a, turned = terms(0)
    first, second = tie([block[-1][0], block[1][0]], own_a[0])
    block[-1], block[1] = [first], [second]
    block[-2], block[2] = [on(first)], [back(second)]

    own_b, others_b = terms(1, 2, deps=(first, second))
    first, second = tie([block[-2][0], block[2][0]], own_b[0])
    block[-2], block[2] = [first], [second]
    block[-3], block[3] = [on(first)], [back(second)]
    exchange((3,), [])

    own_c, others_c = terms(3, deps=(first, second))
    (others_a,) = tie([others_a], own_c[0])
    keep_terms((0,), own_a, others_a)
    up, down = on(term[4][:half]), back(term[4][half:])
    grad_weight = gradient(None, (3,), (own_c[0], term[4]))

    first, second, up, down = tie([block[-3][0], block[3][0], up, down], grad_weight)
    block[-3], block[3] = [first], [second]
    block[4] = [on(first[:half]), back(second[half:])]
    exchange((1, 2), [])
    keep_terms((1, 2), own_b, others_b)
    zero = jnp.zeros((half, part), BF16)
    up, down = add(jnp.concatenate([up, zero], 0), term[3]), add(jnp.concatenate([zero, down], 0), term[-3])
    deps = (up, down)
    up, down = on(up), back(down)
    grad_weight = gradient(grad_weight, (1, 2), deps)

    *block[4], up, down = tie([*block[4], up, down], grad_weight)
    exchange((0,), [])
    keep_terms((3,), own_c, others_c)
    up, down = add(up, term[2]), add(down, term[-2])
    deps = (up, down)
    up, down = on(up), back(down)

    everything = slots(0, 1, 2, 3)
    width = units // 2

    def hidden_phase(start):
        return hidden_gradient(
            places(0, 1, 2, 3), flags(0, 1, 2, 3), everything, code_values, exponents, start, width
        )

    (grad_weight,), (own_left, give) = run([weight_phase(grad_weight, (0,)), hidden_phase(0)], deps, 36 * 1024 * 1024)
    other_left = swap(give)
    up, down = tie([up, down], give)
    up, down = add(up, term[1]), add(down, term[-1])
    deps = (up, down)
    up, down = on(up), back(down)
    ((own_right, give),) = run([hidden_phase(width)], deps)
    other_right = swap(give)
    up, down = tie([up, down], give)
    output_rows = (up.astype(F32) + down.astype(F32) + term[0].astype(F32)).astype(BF16)
    done = finish(gate_input, up_input, own_left, other_left, 0, [], output_rows)
    done = finish(gate_input, up_input, own_right, other_right, width, done)
    return output_rows, done[0], done[1], grad_weight


def any_shards(n, gate_input, up_input, code_values, exponents, cotangent):
    tokens, part = cotangent.shape
    units, features = code_values.shape
    core = lax.axis_index("depth")
    half = n // 2
    gathered = lax.all_gather(cotangent, "grid", axis=0, tiled=False)
    hidden = make_hidden(gate_input, up_input)
    hidden_other = lax.ppermute(hidden, "depth", SWAP)
    place, flag = jnp.zeros((1,), jnp.int32), jnp.ones((1,), jnp.int32)

    (own,), other, turned = output_terms(
        place, hidden, hidden_other, code_values, exponents, features, turn=True
    )
    got = lax.ppermute(other, "depth", SWAP)
    first = jnp.where(core == 0, own, got).reshape(tokens, half, part)
    second = jnp.where(core == 0, got, own).reshape(tokens, half, part)
    pieces = jnp.concatenate([first, second], 1).transpose(1, 0, 2)
    output_rows = lax.psum_scatter(pieces, "grid", scatter_dimension=0, tiled=False)

    keep = lax.dynamic_slice_in_dim(gathered, core * half, half, 0)
    give = lax.dynamic_slice_in_dim(gathered, (1 - core) * half, half, 0)
    both = [keep, lax.ppermute(give, "depth", SWAP)]
    own, other = ([(v.transpose(1, 0, 2).reshape(tokens, features), 0, tokens)] for v in both)
    slots = Slots([[own, own, other]])
    ((grad_mine, grad_give),) = run([hidden_gradient(place, flag, slots, code_values, exponents, 0, units)])
    grad_other = lax.ppermute(grad_give, "depth", SWAP)
    ((grad_weight,),) = run([weight_gradient(place, flag, slots, turned, None, features)])
    grad_gate, grad_up = finish(gate_input, up_input, grad_mine, grad_other, 0, [])
    return output_rows, grad_gate, grad_up, grad_weight


def solution(mesh):
    n = mesh.shape["grid"]
    in_specs = (
        P(("parts", "depth"), "grid"),
        P(("parts", "depth"), "grid"),
        P("grid", "depth"),
        P("grid", "depth"),
        P(("parts", "depth"), "grid"),
    )
    out_specs = (
        P(("parts", "depth"), "grid"),
        P(("parts", "depth"), "grid"),
        P(("parts", "depth"), "grid"),
        P(("parts", "grid"), "depth"),
    )
    step = functools.partial(ring_shards if n == 8 else any_shards, n)
    return jax.shard_map(step, mesh=mesh, in_specs=in_specs, out_specs=out_specs, check_vma=False)
```

```python
import functools

import jax
import jax.numpy as jnp
from jax import lax
from jax.experimental import pallas as pl
from jax.experimental.pallas import tpu as pltpu
from jax.sharding import PartitionSpec as P

F32 = jnp.float32
BF16 = jnp.bfloat16
VMEM_BYTES = 30 * 1024 * 1024
SWAP = [(0, 1), (1, 0)]
ANY = pl.BlockSpec(memory_space=pl.ANY)


def params(size=VMEM_BYTES):
    return pltpu.CompilerParams(vmem_limit_bytes=size)


def cost(flops, size):
    return pl.CostEstimate(flops=flops, bytes_accessed=size, transcendentals=0)


def dequantize(codes, exponents):
    rows, columns = codes.shape
    scale = jnp.exp2(exponents.astype(F32)).astype(BF16)
    blocks = codes.reshape(rows // 32, 32, columns) * scale.reshape(rows // 32, 1, columns)
    return blocks.reshape(rows, columns)


def sigmoid(value):
    return 0.5 * jnp.tanh(0.5 * value) + 0.5


def make_hidden(gate, up):
    tokens, units = gate.shape
    tile = min(units, 1024)
    tiles = units // tile

    def body(g_ref, u_ref, h_ref, gate_held, up_held, out_held, in_sem, out_sem):
        def columns(i):
            return pl.ds(i * tile, tile)

        def store(i):
            return pltpu.make_async_copy(out_held.at[i], h_ref.at[:, columns(i)], out_sem.at[i])

        for i in range(tiles):
            pltpu.make_async_copy(g_ref.at[:, columns(i)], gate_held.at[i], in_sem.at[i, 0]).start()
            pltpu.make_async_copy(u_ref.at[:, columns(i)], up_held.at[i], in_sem.at[i, 1]).start()
        for i in range(tiles):
            wait(gate_held.at[i], in_sem.at[i, 0])
            wait(up_held.at[i], in_sem.at[i, 1])
            value = gate_held[i].astype(F32)
            out_held[i] = (value * sigmoid(value) * up_held[i].astype(F32)).astype(BF16)
            store(i).start()
        for i in range(tiles):
            store(i).wait()

    held = pltpu.VMEM((tiles, tokens, tile), BF16)
    return pl.pallas_call(
        body,
        in_specs=[ANY] * 2,
        out_specs=ANY,
        out_shape=jax.ShapeDtypeStruct((tokens, units), BF16),
        scratch_shapes=[held, held, held, pltpu.SemaphoreType.DMA((tiles, 2)), pltpu.SemaphoreType.DMA((tiles,))],
        compiler_params=params(60 * 1024 * 1024),
        cost_estimate=cost(10 * tokens * units, 6 * tokens * units),
    )(gate, up)


def finish(gate, up, mine, other, first, so_far, *deps):
    tokens, units = gate.shape
    width = mine.shape[1]
    tile = min(width, 1024)
    base = first // tile

    def body(g_ref, u_ref, m_ref, o_ref, *refs):
        dg_ref, du_ref = refs[-2:]
        value = g_ref[...].astype(F32)
        s = sigmoid(value)
        grad = m_ref[...] + o_ref[...].astype(F32)
        slope = s * (1.0 + value * (1.0 - s))
        dg_ref[...] = (grad * u_ref[...].astype(F32) * slope).astype(BF16)
        du_ref[...] = (grad * (value * s)).astype(BF16)

    there = pl.BlockSpec((tokens, tile), lambda i: (0, base + i))
    here = pl.BlockSpec((tokens, tile), lambda i: (0, i))
    shape = jax.ShapeDtypeStruct((tokens, units), BF16)
    return pl.pallas_call(
        body,
        grid=(width // tile,),
        in_specs=[there, there, here, here] + [ANY] * (len(so_far) + len(deps)),
        out_specs=[there] * 2,
        out_shape=[shape] * 2,
        input_output_aliases={4: 0, 5: 1} if so_far else {},
        compiler_params=params(),
        cost_estimate=cost(20000 * tokens * width, 1000 * tokens * width),
    )(gate, up, mine, other, *so_far, *deps)


def block(i, size):
    return pl.ds(pl.multiple_of(i * size, size), size)


def wait(ref, semaphore):
    pltpu.make_async_copy(ref, ref, semaphore).wait()


def output_terms(places, hidden, hidden_other, codes, exponents, part, deps=(), turn=False):
    tokens, units = hidden.shape
    tile = min(part, 512)
    step = min(units, 1024)
    count = places.shape[0]
    tiles = part // tile
    last = count * tiles
    steps = range(0, units, step)
    outputs = 3 if turn else 2

    def body(p_ref, h_ref, x_ref, c_ref, e_ref, *refs):
        out = refs[len(deps) : len(deps) + outputs]
        held, codes_held, exponents_held, out_held, h_sem, c_sem, e_sem, o_sem, *more = refs[len(deps) + outputs :]

        def columns(i):
            return block(p_ref[i // tiles] * tiles + i % tiles, tile)

        def fetch(i, rows, semaphore):
            pltpu.make_async_copy(c_ref.at[rows, columns(i)], codes_held.at[i % 2, rows], semaphore).start()

        def fetch_exponents(i):
            pltpu.make_async_copy(e_ref.at[:, columns(i)], exponents_held.at[i % 2], e_sem.at[i % 2]).start()

        def stores(i):
            rows, lanes = block(i // tiles, tokens), block(i % tiles, tile)
            return [
                pltpu.make_async_copy(out_held.at[i % 2, :tokens], out[0].at[rows, lanes], o_sem.at[i % 2, 0]),
                pltpu.make_async_copy(out_held.at[i % 2, tokens:], out[1].at[rows, lanes], o_sem.at[i % 2, 1]),
            ]

        fetch_exponents(0)
        for n, k in enumerate(steps):
            rows = pl.ds(k, step)
            pltpu.make_async_copy(h_ref.at[:, rows], held.at[:tokens, rows], h_sem.at[n]).start()
            pltpu.make_async_copy(x_ref.at[:, rows], held.at[tokens:, rows], h_sem.at[n]).start()
            fetch(0, rows, c_sem.at[n])
        if last > 1:
            fetch_exponents(1)
            fetch(1, pl.ds(0, units), c_sem.at[len(steps)])

        def work(i):
            wait(exponents_held.at[i % 2], e_sem.at[i % 2])
            total = None
            for n, k in enumerate(steps):
                rows = pl.ds(k, step)
                if isinstance(i, int):
                    wait(held.at[:, rows], h_sem.at[n])
                    wait(codes_held.at[0, rows], c_sem.at[n])
                weight = dequantize(codes_held[i % 2, rows], exponents_held[i % 2, k // 32 : (k + step) // 32, :])
                term = jnp.dot(held[:, rows], weight, preferred_element_type=F32)
                total = term if total is None else total + term
                if turn and isinstance(i, int):
                    turned_held, t_sem = more
                    turned_held[rows] = held[:, rows].T
                    pltpu.make_async_copy(turned_held.at[rows], out[2].at[rows], t_sem.at[n]).start()
            return total.astype(BF16)

        def go_on(i):
            for copy in stores(i):
                copy.start()

            @pl.when(i + 2 < last)
            def _():
                fetch_exponents(i + 2)
                fetch(i + 2, pl.ds(0, units), c_sem.at[len(steps) + (i + 1) % 2])

        out_held[0] = work(0)
        go_on(0)

        @pl.loop(1, last)
        def _(i):
            wait(codes_held.at[i % 2], c_sem.at[len(steps) + (i + 1) % 2])
            total = work(i)

            @pl.when(i >= 2)
            def _():
                for copy in stores(i - 2):
                    copy.wait()

            out_held[i % 2] = total
            go_on(i)

        for i in range(max(0, last - 2), last):
            for copy in stores(i):
                copy.wait()
        if turn:
            turned_held, t_sem = more
            for n, k in enumerate(steps):
                wait(turned_held.at[pl.ds(k, step)], t_sem.at[n])

    out = pl.pallas_call(
        body,
        in_specs=[pl.BlockSpec(memory_space=pltpu.SMEM)] + [ANY] * (4 + len(deps)),
        out_specs=[ANY] * outputs,
        out_shape=[jax.ShapeDtypeStruct((count * tokens, part), BF16)] * 2
        + ([jax.ShapeDtypeStruct((units, 2 * tokens), BF16)] if turn else []),
        scratch_shapes=[
            pltpu.VMEM((2 * tokens, units), BF16),
            pltpu.VMEM((2, units, tile), BF16),
            pltpu.VMEM((2, units // 32, tile), jnp.int32),
            pltpu.VMEM((2, 2 * tokens, tile), BF16),
            pltpu.SemaphoreType.DMA((len(steps),)),
            pltpu.SemaphoreType.DMA((len(steps) + 2,)),
            pltpu.SemaphoreType.DMA((2,)),
            pltpu.SemaphoreType.DMA((2, 2)),
        ]
        + ([pltpu.VMEM((units, 2 * tokens), BF16), pltpu.SemaphoreType.DMA((len(steps),))] if turn else []),
        compiler_params=params(),
        cost_estimate=cost(4 * tokens * units * part * count, 2 * units * part * count),
    )(places, hidden, hidden_other, codes, exponents, *deps)
    return out


class Slots:
    def __init__(self, blocks):
        self.blocks = blocks
        self.arrays = [piece[0] for block in blocks for rows in block for piece in rows]
        self.tokens = sum(piece[2] for piece in blocks[0][2])
        self.part = blocks[0][2][0][0].shape[1]

    def scratch(self):
        return [
            pltpu.VMEM((len(self.blocks), 2 * self.tokens, self.part), BF16),
            pltpu.SemaphoreType.DMA((len(self.blocks),)),
        ]

    def load(self, j, flags, refs, held, semaphores):
        before = sum(len(rows) for block in self.blocks[:j] for rows in block)
        refs = iter(refs[before:])
        for wanted, rows in zip((1, 0, None), self.blocks[j]):
            copies, row = [], self.tokens if wanted is None else 0
            for _, first, size in rows:
                copies.append(
                    pltpu.make_async_copy(
                        next(refs).at[pl.ds(first, size)], held.at[j, pl.ds(row, size)], semaphores.at[j]
                    )
                )
                row += size

            def start(copies=copies):
                for copy in copies:
                    copy.start()

            if wanted is None:
                start()
            else:
                pl.when(flags[j] == wanted)(start)


def run(phases, deps=(), size=VMEM_BYTES):
    smem = pl.BlockSpec(memory_space=pltpu.SMEM)
    ends = []
    aliases = {}
    given, made, held = 0, 0, 0
    for phase in phases:
        for i, o in phase["aliases"].items():
            aliases[given + i] = made + o
        ends.append((given, made, held))
        given += phase["scalars"] + len(phase["inputs"])
        made += len(phase["shapes"])
        held += len(phase["scratch"])
    ends.append((given, made, held))

    def body(*refs):
        inputs, outputs = refs[:given], refs[given + len(deps) : given + len(deps) + made]
        scratch = refs[given + len(deps) + made :]
        steps = []
        for phase, (i, o, h), (i_end, o_end, h_end) in zip(phases, ends, ends[1:]):
            steps.append(phase["body"](*inputs[i:i_end], *outputs[o:o_end], *scratch[h:h_end]))
        for step in steps:
            next(step)
        for step in steps:
            next(step, None)

    out = pl.pallas_call(
        body,
        in_specs=[
            spec for p in phases for spec in [smem] * p["scalars"] + [ANY] * len(p["inputs"])
        ]
        + [ANY] * len(deps),
        out_specs=[ANY] * made,
        out_shape=[shape for p in phases for shape in p["shapes"]],
        input_output_aliases=aliases,
        scratch_shapes=[shape for p in phases for shape in p["scratch"]],
        compiler_params=params(size),
        cost_estimate=cost(sum(p["flops"] for p in phases), sum(p["size"] for p in phases)),
    )(*[value for p in phases for value in p["numbers"] + p["inputs"]], *deps)
    return [out[a[1] : b[1]] for a, b in zip(ends, ends[1:])]


def hidden_gradient(places, flags, slots, codes, exponents, first, width, alone=True):
    tokens, part, count = slots.tokens, slots.part, len(slots.blocks)
    tile = min(width, 512)
    tiles = width // tile
    given = len(slots.arrays)
    step = min(part, 1024)

    def body(p_ref, f_ref, *refs):
        c_ref, e_ref = refs[given : given + 2]
        m_ref, o_ref, held, t_sem, codes_held, exponents_held, m_held, o_held, c_sem, e_sem, o_sem = refs[given + 2 :]

        def columns(j):
            return pl.ds(pl.multiple_of(p_ref[j] * part, part), part)

        def fetch(i, j):
            rows = pl.ds(first + pl.multiple_of(i * tile, tile), tile)
            pltpu.make_async_copy(c_ref.at[rows, columns(j)], codes_held.at[i % 2, j], c_sem.at[i % 2, j]).start()

        def stores(i):
            lanes = block(i, tile)
            return [
                pltpu.make_async_copy(m_held.at[i % 2], m_ref.at[:, lanes], o_sem.at[i % 2, 0]),
                pltpu.make_async_copy(o_held.at[i % 2], o_ref.at[:, lanes], o_sem.at[i % 2, 1]),
            ]

        for j in range(count):
            slots.load(j, f_ref, refs[:given], held, t_sem)
            fetch(0, j)
            rows = pl.ds(first // 32, width // 32)
            pltpu.make_async_copy(e_ref.at[rows, columns(j)], exponents_held.at[j], e_sem.at[j]).start()
        if tiles > 1:
            for j in range(count):
                fetch(1, j)
        yield

        def arrive(j):
            wait(held.at[j], t_sem.at[j])
            wait(exponents_held.at[j], e_sem.at[j])

        def work(i, step_by_step):
            if not step_by_step:
                for j in range(count):
                    wait(codes_held.at[i % 2, j], c_sem.at[i % 2, j])
            total = None
            for j in range(count):
                if step_by_step:
                    arrive(j)
                    wait(codes_held.at[i % 2, j], c_sem.at[i % 2, j])
                for k in range(0, part, step):
                    lanes = pl.ds(k, step)
                    weight = dequantize(
                        codes_held[i % 2, j, :, lanes], exponents_held[j, block(i, tile // 32), lanes]
                    )
                    term = lax.dot_general(
                        held[j, :, lanes], weight, (((1,), (1,)), ((), ())), preferred_element_type=F32
                    )
                    total = term if total is None else total + term

            @pl.when(i >= 2)
            def _():
                for copy in stores(i - 2):
                    copy.wait()

            m_held[i % 2] = total[:tokens]
            o_held[i % 2] = total[tokens:].astype(BF16)
            for copy in stores(i):
                copy.start()

            @pl.when(i + 2 < tiles)
            def _():
                for j in range(count):
                    fetch(i + 2, j)

        if alone:
            work(0, True)
        else:
            for j in range(count):
                arrive(j)

        @pl.loop(1 if alone else 0, tiles)
        def _(i):
            work(i, False)

        for i in range(max(0, tiles - 2), tiles):
            for copy in stores(i):
                copy.wait()

    return dict(
        body=body,
        scalars=2,
        numbers=[places, flags],
        inputs=[*slots.arrays, codes, exponents],
        shapes=[jax.ShapeDtypeStruct((tokens, width), F32), jax.ShapeDtypeStruct((tokens, width), BF16)],
        aliases={},
        scratch=slots.scratch()
        + [
            pltpu.VMEM((2, count, tile, part), BF16),
            pltpu.VMEM((count, width // 32, part), jnp.int32),
            pltpu.VMEM((2, tokens, tile), F32),
            pltpu.VMEM((2, tokens, tile), BF16),
            pltpu.SemaphoreType.DMA((2, count)),
            pltpu.SemaphoreType.DMA((count,)),
            pltpu.SemaphoreType.DMA((2, 2)),
        ],
        flops=4 * tokens * width * part * count,
        size=2 * width * part * count,
    )


def weight_gradient(places, flags, slots, turned, so_far, features):
    part, count = slots.part, len(slots.blocks)
    units, rows_all = turned.shape
    tile = min(units, 512)
    tiles = units // tile
    given = len(slots.arrays)
    step = min(part, 1024)
    ahead = min(4, tiles)
    behind = min(4, tiles)

    def body(p_ref, f_ref, *refs):
        h_ref = refs[given]
        w_ref, held, t_sem, turned_held, out_held, h_sem, o_sem = refs[-7:]

        def fetch(i):
            slot = i % ahead
            pltpu.make_async_copy(h_ref.at[block(i, tile)], turned_held.at[slot], h_sem.at[slot]).start()

        def store(i, j):
            columns = pl.ds(pl.multiple_of(p_ref[j] * part, part), part)
            return pltpu.make_async_copy(
                out_held.at[i % behind, j], w_ref.at[block(i, tile), columns], o_sem.at[i % behind, j]
            )

        fetch(0)
        for j in range(count):
            slots.load(j, f_ref, refs[:given], held, t_sem)
        for i in range(1, ahead):
            fetch(i)
        yield

        @pl.loop(0, tiles)
        def _(i):
            wait(turned_held.at[i % ahead], h_sem.at[i % ahead])
            left = turned_held[i % ahead]

            @pl.when(i >= behind)
            def _():
                for j in range(count):
                    store(i - behind, j).wait()

            for j in range(count):

                @pl.when(i == 0)
                def _(j=j):
                    wait(held.at[j], t_sem.at[j])

                for k in range(0, part, step):
                    lanes = pl.ds(k, step)
                    out_held[i % behind, j, :, lanes] = jnp.dot(
                        left, held[j, :, lanes], preferred_element_type=F32
                    ).astype(BF16)
                store(i, j).start()

            @pl.when(i + ahead < tiles)
            def _():
                fetch(i + ahead)

        for i in range(tiles - behind, tiles):
            for j in range(count):
                store(i, j).wait()

    extra = [] if so_far is None else [so_far]
    return dict(
        body=body,
        scalars=2,
        numbers=[places, flags],
        inputs=[*slots.arrays, turned, *extra],
        shapes=[jax.ShapeDtypeStruct((units, features), BF16)],
        aliases={3 + given: 0} if extra else {},
        scratch=slots.scratch()
        + [
            pltpu.VMEM((ahead, tile, rows_all), BF16),
            pltpu.VMEM((behind, count, tile, part), BF16),
            pltpu.SemaphoreType.DMA((ahead,)),
            pltpu.SemaphoreType.DMA((behind, count)),
        ],
        flops=2 * rows_all * units * part * count,
        size=2 * units * part * count,
    )


def tie(values, *deps):
    count = len(values)

    def body(*refs):
        pass

    return pl.pallas_call(
        body,
        in_specs=[ANY] * (count + len(deps)),
        out_specs=[ANY] * count,
        out_shape=[jax.ShapeDtypeStruct(v.shape, v.dtype) for v in values],
        input_output_aliases={i: i for i in range(count)},
        compiler_params=params(),
    )(*values, *deps)


def choose(flags, pairs, values, deps):
    arrays = [piece for pair in pairs for block in pair for piece in block]
    tokens, part = sum(p.shape[0] for p in pairs[0][0]), pairs[0][0][0].shape[1]
    count, kept = len(arrays), len(values)

    def body(f_ref, *refs):
        o_ref, semaphore = refs[-2 - kept], refs[-1]
        given = iter(refs[:count])
        for j, pair in enumerate(pairs):
            for wanted, block in zip((1, 0), pair):
                copies, row = [], j * tokens
                for piece in block:
                    size = piece.shape[0]
                    copies.append(pltpu.make_async_copy(next(given), o_ref.at[pl.ds(row, size)], semaphore))
                    row += size

                @pl.when(f_ref[j] == wanted)
                def _(copies=copies):
                    for copy in copies:
                        copy.start()

        pltpu.make_async_copy(o_ref, o_ref, semaphore).wait()

    return pl.pallas_call(
        body,
        in_specs=[pl.BlockSpec(memory_space=pltpu.SMEM)] + [ANY] * (count + kept + len(deps)),
        out_specs=[ANY] * (1 + kept),
        out_shape=[jax.ShapeDtypeStruct((len(pairs) * tokens, part), BF16)]
        + [jax.ShapeDtypeStruct(v.shape, v.dtype) for v in values],
        input_output_aliases={1 + count + i: 1 + i for i in range(kept)},
        scratch_shapes=[pltpu.SemaphoreType.DMA],
        compiler_params=params(),
    )(flags, *arrays, *values, *deps)


def ring_shards(n, gate_input, up_input, code_values, exponents, cotangent):
    tokens, part = cotangent.shape
    units, features = code_values.shape
    lines = n // 2
    ring = [2 * p for p in range(lines)] + [2 * (n - 1 - p) + 1 for p in range(lines, n)]
    forward = [(ring[p], ring[(p + 1) % n]) for p in range(n)]
    backward = [(b, a) for a, b in forward]
    core = lax.axis_index("depth")
    index = lax.axis_index("grid")
    line = index // 2
    here = jnp.where(index % 2 == 0, line, n - 1 - line)

    def owner(offset):
        p = (here + offset + n) % n
        return jnp.where(p < lines, 2 * p, 2 * (n - 1 - p) + 1)

    def swap(value):
        return lax.ppermute(value, "depth", SWAP)

    def on(value):
        return lax.ppermute(value, "grid", forward)

    def back(value):
        return lax.ppermute(value, "grid", backward)

    pairs = [(4, 0), (3, -1), (-3, 1), (2, -2)]
    mine = [owner(a) // lines == core for a, _ in pairs]
    place = [jnp.where(m, owner(a), owner(b)) % lines for (a, b), m in zip(pairs, mine)]

    def places(*group):
        return jnp.stack([place[j] for j in group]).astype(jnp.int32)

    def flags(*group):
        return jnp.stack([mine[j] for j in group]).astype(jnp.int32)

    half = tokens // 2
    block, got, term = {0: [cotangent]}, {}, {}

    def pieces(rows):
        return [(piece, 0, piece.shape[0]) for piece in rows]

    def terms(*group, deps=()):
        own, others, *turned = output_terms(
            places(*group), hidden, hidden_other, code_values, exponents, part, deps, group == (0,)
        )
        return own, swap(others), *turned

    def keep_terms(group, own, others):
        for i, j in enumerate(group):
            a, b = pairs[j]
            here, there = (rows[i * tokens : (i + 1) * tokens] for rows in (own, others))
            term[a] = jnp.where(mine[j], here, there)
            term[b] = jnp.where(mine[j], there, here)

    def slots(*group):
        return Slots([[pieces(block[a]), pieces(block[b]), got[j]] for j in group for a, b in (pairs[j],)])

    def weight_phase(so_far, group):
        return weight_gradient(places(*group), flags(*group), slots(*group), turned, so_far, features)

    def gradient(so_far, group, deps=()):
        (((out,)),) = run([weight_phase(so_far, group)], deps)
        return out

    def add(value, other):
        return (value.astype(F32) + other.astype(F32)).astype(BF16)

    def exchange(group, values, *deps):
        chosen = [(block[pairs[j][1]], block[pairs[j][0]]) for j in group]
        given, *values = choose(flags(*group), chosen, values, deps)
        found = swap(given)
        for i, j in enumerate(group):
            got[j] = [(found, i * tokens, tokens)]
        return values

    block[-1], block[1] = [on(cotangent)], [back(cotangent)]
    hidden = make_hidden(gate_input, up_input)
    hidden_other = swap(hidden)

    own_a, others_a, turned = terms(0)
    first, second = tie([block[-1][0], block[1][0]], own_a)
    block[-1], block[1] = [first], [second]
    block[-2], block[2] = [on(first)], [back(second)]

    own_b, others_b = terms(1, 2, deps=(first, second))
    first, second = tie([block[-2][0], block[2][0]], own_b)
    block[-2], block[2] = [first], [second]
    block[-3], block[3] = [on(first)], [back(second)]
    exchange((3,), [])

    own_c, others_c = terms(3, deps=(first, second))
    (others_a,) = tie([others_a], own_c)
    keep_terms((0,), own_a, others_a)
    up, down = on(term[4][:half]), back(term[4][half:])
    grad_weight = gradient(None, (3,), (own_c, term[4]))

    first, second, up, down = tie([block[-3][0], block[3][0], up, down], grad_weight)
    block[-3], block[3] = [first], [second]
    block[4] = [on(first[:half]), back(second[half:])]
    exchange((1, 2), [])
    keep_terms((1, 2), own_b, others_b)
    zero = jnp.zeros((half, part), BF16)
    up, down = add(jnp.concatenate([up, zero], 0), term[3]), add(jnp.concatenate([zero, down], 0), term[-3])
    deps = (up, down)
    up, down = on(up), back(down)
    grad_weight = gradient(grad_weight, (1, 2), deps)

    *block[4], up, down = tie([*block[4], up, down], grad_weight)
    exchange((0,), [])
    keep_terms((3,), own_c, others_c)
    up, down = add(up, term[2]), add(down, term[-2])
    deps = (up, down)
    up, down = on(up), back(down)

    everything = slots(0, 1, 2, 3)
    width = units // 2

    def hidden_phase(start, alone):
        return hidden_gradient(
            places(0, 1, 2, 3), flags(0, 1, 2, 3), everything, code_values, exponents, start, width, alone
        )

    (grad_weight,), (own_left, give) = run([weight_phase(grad_weight, (0,)), hidden_phase(0, False)], deps, 36 * 1024 * 1024)
    other_left = swap(give)
    up, down = tie([up, down], give)
    up, down = add(up, term[1]), add(down, term[-1])
    deps = (up, down)
    up, down = on(up), back(down)
    ((own_right, give),) = run([hidden_phase(width, True)], deps)
    other_right = swap(give)
    up, down = tie([up, down], give)
    output_rows = (up.astype(F32) + down.astype(F32) + term[0].astype(F32)).astype(BF16)
    done = finish(gate_input, up_input, own_left, other_left, 0, [], output_rows)
    done = finish(gate_input, up_input, own_right, other_right, width, done)
    return output_rows, done[0], done[1], grad_weight


def any_shards(n, gate_input, up_input, code_values, exponents, cotangent):
    tokens, part = cotangent.shape
    units, features = code_values.shape
    core = lax.axis_index("depth")
    half = n // 2
    gathered = lax.all_gather(cotangent, "grid", axis=0, tiled=False)
    hidden = make_hidden(gate_input, up_input)
    hidden_other = lax.ppermute(hidden, "depth", SWAP)
    place, flag = jnp.zeros((1,), jnp.int32), jnp.ones((1,), jnp.int32)

    own, other, turned = output_terms(
        place, hidden, hidden_other, code_values, exponents, features, turn=True
    )
    got = lax.ppermute(other, "depth", SWAP)
    first = jnp.where(core == 0, own, got).reshape(tokens, half, part)
    second = jnp.where(core == 0, got, own).reshape(tokens, half, part)
    pieces = jnp.concatenate([first, second], 1).transpose(1, 0, 2)
    output_rows = lax.psum_scatter(pieces, "grid", scatter_dimension=0, tiled=False)

    keep = lax.dynamic_slice_in_dim(gathered, core * half, half, 0)
    give = lax.dynamic_slice_in_dim(gathered, (1 - core) * half, half, 0)
    both = [keep, lax.ppermute(give, "depth", SWAP)]
    own, other = ([(v.transpose(1, 0, 2).reshape(tokens, features), 0, tokens)] for v in both)
    slots = Slots([[own, own, other]])
    ((grad_mine, grad_give),) = run([hidden_gradient(place, flag, slots, code_values, exponents, 0, units)])
    grad_other = lax.ppermute(grad_give, "depth", SWAP)
    ((grad_weight,),) = run([weight_gradient(place, flag, slots, turned, None, features)])
    grad_gate, grad_up = finish(gate_input, up_input, grad_mine, grad_other, 0, [])
    return output_rows, grad_gate, grad_up, grad_weight


def solution(mesh):
    n = mesh.shape["grid"]
    in_specs = (
        P(("parts", "depth"), "grid"),
        P(("parts", "depth"), "grid"),
        P("grid", "depth"),
        P("grid", "depth"),
        P(("parts", "depth"), "grid"),
    )
    out_specs = (
        P(("parts", "depth"), "grid"),
        P(("parts", "depth"), "grid"),
        P(("parts", "depth"), "grid"),
        P(("parts", "grid"), "depth"),
    )
    step = functools.partial(ring_shards if n == 8 else any_shards, n)
    return jax.shard_map(step, mesh=mesh, in_specs=in_specs, out_specs=out_specs, check_vma=False)
```

```python
import functools

import jax
import jax.numpy as jnp
from jax import lax
from jax.experimental import pallas as pl
from jax.experimental.pallas import tpu as pltpu
from jax.sharding import PartitionSpec as P

F32 = jnp.float32
BF16 = jnp.bfloat16
VMEM_BYTES = 30 * 1024 * 1024
SWAP = [(0, 1), (1, 0)]
ANY = pl.BlockSpec(memory_space=pl.ANY)


def params(size=VMEM_BYTES):
    return pltpu.CompilerParams(vmem_limit_bytes=size)


def cost(flops, size):
    return pl.CostEstimate(flops=flops, bytes_accessed=size, transcendentals=0)


def dequantize(codes, exponents):
    rows, columns = codes.shape
    scale = jnp.exp2(exponents.astype(F32)).astype(BF16)
    blocks = codes.reshape(rows // 32, 32, columns) * scale.reshape(rows // 32, 1, columns)
    return blocks.reshape(rows, columns)


def sigmoid(value):
    return 0.5 * jnp.tanh(0.5 * value) + 0.5


def make_hidden(gate, up):
    tokens, units = gate.shape
    tile = min(units, 1024)
    tiles = units // tile

    def body(g_ref, u_ref, h_ref, gate_held, up_held, out_held, in_sem, out_sem):
        def columns(i):
            return pl.ds(i * tile, tile)

        def store(i):
            return pltpu.make_async_copy(out_held.at[i], h_ref.at[:, columns(i)], out_sem.at[i])

        for i in range(tiles):
            pltpu.make_async_copy(g_ref.at[:, columns(i)], gate_held.at[i], in_sem.at[i, 0]).start()
            pltpu.make_async_copy(u_ref.at[:, columns(i)], up_held.at[i], in_sem.at[i, 1]).start()
        for i in range(tiles):
            wait(gate_held.at[i], in_sem.at[i, 0])
            wait(up_held.at[i], in_sem.at[i, 1])
            value = gate_held[i].astype(F32)
            out_held[i] = (value * sigmoid(value) * up_held[i].astype(F32)).astype(BF16)
            store(i).start()
        for i in range(tiles):
            store(i).wait()

    held = pltpu.VMEM((tiles, tokens, tile), BF16)
    return pl.pallas_call(
        body,
        in_specs=[ANY] * 2,
        out_specs=ANY,
        out_shape=jax.ShapeDtypeStruct((tokens, units), BF16),
        scratch_shapes=[held, held, held, pltpu.SemaphoreType.DMA((tiles, 2)), pltpu.SemaphoreType.DMA((tiles,))],
        compiler_params=params(60 * 1024 * 1024),
        cost_estimate=cost(10 * tokens * units, 6 * tokens * units),
    )(gate, up)


def finish(gate, up, mine, other, first, so_far, *deps):
    tokens, units = gate.shape
    width = mine.shape[1]
    tile = min(width, 1024)
    base = first // tile

    def body(g_ref, u_ref, m_ref, o_ref, *refs):
        dg_ref, du_ref = refs[-2:]
        value = g_ref[...].astype(F32)
        s = sigmoid(value)
        grad = m_ref[...] + o_ref[...].astype(F32)
        slope = s * (1.0 + value * (1.0 - s))
        dg_ref[...] = (grad * u_ref[...].astype(F32) * slope).astype(BF16)
        du_ref[...] = (grad * (value * s)).astype(BF16)

    there = pl.BlockSpec((tokens, tile), lambda i: (0, base + i))
    here = pl.BlockSpec((tokens, tile), lambda i: (0, i))
    shape = jax.ShapeDtypeStruct((tokens, units), BF16)
    return pl.pallas_call(
        body,
        grid=(width // tile,),
        in_specs=[there, there, here, here] + [ANY] * (len(so_far) + len(deps)),
        out_specs=[there] * 2,
        out_shape=[shape] * 2,
        input_output_aliases={4: 0, 5: 1} if so_far else {},
        compiler_params=params(),
        cost_estimate=cost(20000 * tokens * width, 1000 * tokens * width),
    )(gate, up, mine, other, *so_far, *deps)


def block(i, size):
    return pl.ds(pl.multiple_of(i * size, size), size)


def wait(ref, semaphore):
    pltpu.make_async_copy(ref, ref, semaphore).wait()


def output_terms(places, hidden, hidden_other, codes, exponents, part, deps=(), turn=False):
    tokens, units = hidden.shape
    tile = min(part, 512)
    step = min(units, 1024)
    count = places.shape[0]
    tiles = part // tile
    last = count * tiles
    steps = range(0, units, step)
    outputs = 3 if turn else 2

    def body(p_ref, h_ref, x_ref, c_ref, e_ref, *refs):
        out = refs[len(deps) : len(deps) + outputs]
        held, codes_held, exponents_held, out_held, h_sem, c_sem, e_sem, o_sem, *more = refs[len(deps) + outputs :]

        def columns(i):
            return block(p_ref[i // tiles] * tiles + i % tiles, tile)

        def fetch(i, rows, semaphore):
            pltpu.make_async_copy(c_ref.at[rows, columns(i)], codes_held.at[i % 2, rows], semaphore).start()

        def fetch_exponents(i):
            pltpu.make_async_copy(e_ref.at[:, columns(i)], exponents_held.at[i % 2], e_sem.at[i % 2]).start()

        def stores(i):
            rows, lanes = block(i // tiles, tokens), block(i % tiles, tile)
            return [
                pltpu.make_async_copy(out_held.at[i % 2, :tokens], out[0].at[rows, lanes], o_sem.at[i % 2, 0]),
                pltpu.make_async_copy(out_held.at[i % 2, tokens:], out[1].at[rows, lanes], o_sem.at[i % 2, 1]),
            ]

        fetch_exponents(0)
        for n, k in enumerate(steps):
            rows = pl.ds(k, step)
            pltpu.make_async_copy(h_ref.at[:, rows], held.at[:tokens, rows], h_sem.at[n]).start()
            pltpu.make_async_copy(x_ref.at[:, rows], held.at[tokens:, rows], h_sem.at[n]).start()
            fetch(0, rows, c_sem.at[n])
        if last > 1:
            fetch_exponents(1)
            fetch(1, pl.ds(0, units), c_sem.at[len(steps)])

        def work(i):
            wait(exponents_held.at[i % 2], e_sem.at[i % 2])
            total = None
            for n, k in enumerate(steps):
                rows = pl.ds(k, step)
                if isinstance(i, int):
                    wait(held.at[:, rows], h_sem.at[n])
                    wait(codes_held.at[0, rows], c_sem.at[n])
                weight = dequantize(codes_held[i % 2, rows], exponents_held[i % 2, k // 32 : (k + step) // 32, :])
                term = jnp.dot(held[:, rows], weight, preferred_element_type=F32)
                total = term if total is None else total + term
                if turn and isinstance(i, int):
                    turned_held, t_sem = more
                    turned_held[rows] = held[:, rows].T
                    pltpu.make_async_copy(turned_held.at[rows], out[2].at[rows], t_sem.at[n]).start()
            return total.astype(BF16)

        def go_on(i):
            for copy in stores(i):
                copy.start()

            @pl.when(i + 2 < last)
            def _():
                fetch_exponents(i + 2)
                fetch(i + 2, pl.ds(0, units), c_sem.at[len(steps) + (i + 1) % 2])

        out_held[0] = work(0)
        go_on(0)

        @pl.loop(1, last)
        def _(i):
            wait(codes_held.at[i % 2], c_sem.at[len(steps) + (i + 1) % 2])
            total = work(i)

            @pl.when(i >= 2)
            def _():
                for copy in stores(i - 2):
                    copy.wait()

            out_held[i % 2] = total
            go_on(i)

        for i in range(max(0, last - 2), last):
            for copy in stores(i):
                copy.wait()
        if turn:
            turned_held, t_sem = more
            for n, k in enumerate(steps):
                wait(turned_held.at[pl.ds(k, step)], t_sem.at[n])

    out = pl.pallas_call(
        body,
        in_specs=[pl.BlockSpec(memory_space=pltpu.SMEM)] + [ANY] * (4 + len(deps)),
        out_specs=[ANY] * outputs,
        out_shape=[jax.ShapeDtypeStruct((count * tokens, part), BF16)] * 2
        + ([jax.ShapeDtypeStruct((units, 2 * tokens), BF16)] if turn else []),
        scratch_shapes=[
            pltpu.VMEM((2 * tokens, units), BF16),
            pltpu.VMEM((2, units, tile), BF16),
            pltpu.VMEM((2, units // 32, tile), jnp.int32),
            pltpu.VMEM((2, 2 * tokens, tile), BF16),
            pltpu.SemaphoreType.DMA((len(steps),)),
            pltpu.SemaphoreType.DMA((len(steps) + 2,)),
            pltpu.SemaphoreType.DMA((2,)),
            pltpu.SemaphoreType.DMA((2, 2)),
        ]
        + ([pltpu.VMEM((units, 2 * tokens), BF16), pltpu.SemaphoreType.DMA((len(steps),))] if turn else []),
        compiler_params=params(),
        cost_estimate=cost(4 * tokens * units * part * count, 2 * units * part * count),
    )(places, hidden, hidden_other, codes, exponents, *deps)
    return out


class Slots:
    def __init__(self, blocks):
        self.blocks = blocks
        self.arrays = [piece[0] for block in blocks for rows in block for piece in rows]
        self.tokens = sum(piece[2] for piece in blocks[0][2])
        self.part = blocks[0][2][0][0].shape[1]

    def scratch(self):
        return [
            pltpu.VMEM((len(self.blocks), 2 * self.tokens, self.part), BF16),
            pltpu.SemaphoreType.DMA((len(self.blocks),)),
        ]

    def load(self, j, flags, refs, held, semaphores):
        before = sum(len(rows) for block in self.blocks[:j] for rows in block)
        refs = iter(refs[before:])
        for wanted, rows in zip((1, 0, None), self.blocks[j]):
            copies, row = [], self.tokens if wanted is None else 0
            for _, first, size in rows:
                copies.append(
                    pltpu.make_async_copy(
                        next(refs).at[pl.ds(first, size)], held.at[j, pl.ds(row, size)], semaphores.at[j]
                    )
                )
                row += size

            def start(copies=copies):
                for copy in copies:
                    copy.start()

            if wanted is None:
                start()
            else:
                pl.when(flags[j] == wanted)(start)


def run(phases, deps=(), size=VMEM_BYTES):
    smem = pl.BlockSpec(memory_space=pltpu.SMEM)
    ends = []
    aliases = {}
    given, made, held = 0, 0, 0
    for phase in phases:
        for i, o in phase["aliases"].items():
            aliases[given + i] = made + o
        ends.append((given, made, held))
        given += phase["scalars"] + len(phase["inputs"])
        made += len(phase["shapes"])
        held += len(phase["scratch"])
    ends.append((given, made, held))

    def body(*refs):
        inputs, outputs = refs[:given], refs[given + len(deps) : given + len(deps) + made]
        scratch = refs[given + len(deps) + made :]
        steps = []
        for phase, (i, o, h), (i_end, o_end, h_end) in zip(phases, ends, ends[1:]):
            steps.append(phase["body"](*inputs[i:i_end], *outputs[o:o_end], *scratch[h:h_end]))
        for step in steps:
            next(step)
        for step in steps:
            next(step, None)

    out = pl.pallas_call(
        body,
        in_specs=[
            spec for p in phases for spec in [smem] * p["scalars"] + [ANY] * len(p["inputs"])
        ]
        + [ANY] * len(deps),
        out_specs=[ANY] * made,
        out_shape=[shape for p in phases for shape in p["shapes"]],
        input_output_aliases=aliases,
        scratch_shapes=[shape for p in phases for shape in p["scratch"]],
        compiler_params=params(size),
        cost_estimate=cost(sum(p["flops"] for p in phases), sum(p["size"] for p in phases)),
    )(*[value for p in phases for value in p["numbers"] + p["inputs"]], *deps)
    return [out[a[1] : b[1]] for a, b in zip(ends, ends[1:])]


def hidden_gradient(places, flags, slots, codes, exponents, first, width, alone=True):
    tokens, part, count = slots.tokens, slots.part, len(slots.blocks)
    tile = min(width, 512)
    tiles = width // tile
    given = len(slots.arrays)
    step = min(part, 1024)

    def body(p_ref, f_ref, *refs):
        c_ref, e_ref = refs[given : given + 2]
        m_ref, o_ref, held, t_sem, codes_held, exponents_held, m_held, o_held, c_sem, e_sem, o_sem = refs[given + 2 :]

        def columns(j):
            return pl.ds(pl.multiple_of(p_ref[j] * part, part), part)

        def fetch(i, j):
            rows = pl.ds(first + pl.multiple_of(i * tile, tile), tile)
            pltpu.make_async_copy(c_ref.at[rows, columns(j)], codes_held.at[i % 2, j], c_sem.at[i % 2, j]).start()

        def stores(i):
            lanes = block(i, tile)
            return [
                pltpu.make_async_copy(m_held.at[i % 2], m_ref.at[:, lanes], o_sem.at[i % 2, 0]),
                pltpu.make_async_copy(o_held.at[i % 2], o_ref.at[:, lanes], o_sem.at[i % 2, 1]),
            ]

        for j in range(count):
            slots.load(j, f_ref, refs[:given], held, t_sem)
            fetch(0, j)
            rows = pl.ds(first // 32, width // 32)
            pltpu.make_async_copy(e_ref.at[rows, columns(j)], exponents_held.at[j], e_sem.at[j]).start()
        if tiles > 1:
            for j in range(count):
                fetch(1, j)
        yield

        def arrive(j):
            wait(held.at[j], t_sem.at[j])
            wait(exponents_held.at[j], e_sem.at[j])

        def work(i, step_by_step):
            if not step_by_step:
                for j in range(count):
                    wait(codes_held.at[i % 2, j], c_sem.at[i % 2, j])
            total = None
            for j in range(count):
                if step_by_step:
                    arrive(j)
                    wait(codes_held.at[i % 2, j], c_sem.at[i % 2, j])
                for k in range(0, part, step):
                    lanes = pl.ds(k, step)
                    weight = dequantize(
                        codes_held[i % 2, j, :, lanes], exponents_held[j, block(i, tile // 32), lanes]
                    )
                    term = lax.dot_general(
                        held[j, :, lanes], weight, (((1,), (1,)), ((), ())), preferred_element_type=F32
                    )
                    total = term if total is None else total + term

            @pl.when(i >= 2)
            def _():
                for copy in stores(i - 2):
                    copy.wait()

            m_held[i % 2] = total[:tokens]
            o_held[i % 2] = total[tokens:].astype(BF16)
            for copy in stores(i):
                copy.start()

            @pl.when(i + 2 < tiles)
            def _():
                for j in range(count):
                    fetch(i + 2, j)

        if alone:
            work(0, True)
        else:
            for j in range(count):
                arrive(j)

        @pl.loop(1 if alone else 0, tiles)
        def _(i):
            work(i, False)

        for i in range(max(0, tiles - 2), tiles):
            for copy in stores(i):
                copy.wait()

    return dict(
        body=body,
        scalars=2,
        numbers=[places, flags],
        inputs=[*slots.arrays, codes, exponents],
        shapes=[jax.ShapeDtypeStruct((tokens, width), F32), jax.ShapeDtypeStruct((tokens, width), BF16)],
        aliases={},
        scratch=slots.scratch()
        + [
            pltpu.VMEM((2, count, tile, part), BF16),
            pltpu.VMEM((count, width // 32, part), jnp.int32),
            pltpu.VMEM((2, tokens, tile), F32),
            pltpu.VMEM((2, tokens, tile), BF16),
            pltpu.SemaphoreType.DMA((2, count)),
            pltpu.SemaphoreType.DMA((count,)),
            pltpu.SemaphoreType.DMA((2, 2)),
        ],
        flops=4 * tokens * width * part * count,
        size=2 * width * part * count,
    )


def weight_gradient(places, flags, slots, turned, so_far, features):
    part, count = slots.part, len(slots.blocks)
    units, rows_all = turned.shape
    tile = min(units, 512)
    tiles = units // tile
    given = len(slots.arrays)
    step = min(part, 1024)
    ahead = min(4, tiles)
    behind = min(4, tiles)

    def body(p_ref, f_ref, *refs):
        h_ref = refs[given]
        w_ref, held, t_sem, turned_held, out_held, h_sem, o_sem = refs[-7:]

        def fetch(i):
            slot = i % ahead
            pltpu.make_async_copy(h_ref.at[block(i, tile)], turned_held.at[slot], h_sem.at[slot]).start()

        def store(i, j):
            columns = pl.ds(pl.multiple_of(p_ref[j] * part, part), part)
            return pltpu.make_async_copy(
                out_held.at[i % behind, j], w_ref.at[block(i, tile), columns], o_sem.at[i % behind, j]
            )

        fetch(0)
        for j in range(count):
            slots.load(j, f_ref, refs[:given], held, t_sem)
        for i in range(1, ahead):
            fetch(i)
        yield

        @pl.loop(0, tiles)
        def _(i):
            wait(turned_held.at[i % ahead], h_sem.at[i % ahead])
            left = turned_held[i % ahead]

            @pl.when(i >= behind)
            def _():
                for j in range(count):
                    store(i - behind, j).wait()

            for j in range(count):

                @pl.when(i == 0)
                def _(j=j):
                    wait(held.at[j], t_sem.at[j])

                for k in range(0, part, step):
                    lanes = pl.ds(k, step)
                    out_held[i % behind, j, :, lanes] = jnp.dot(
                        left, held[j, :, lanes], preferred_element_type=F32
                    ).astype(BF16)
                store(i, j).start()

            @pl.when(i + ahead < tiles)
            def _():
                fetch(i + ahead)

        for i in range(tiles - behind, tiles):
            for j in range(count):
                store(i, j).wait()

    extra = [] if so_far is None else [so_far]
    return dict(
        body=body,
        scalars=2,
        numbers=[places, flags],
        inputs=[*slots.arrays, turned, *extra],
        shapes=[jax.ShapeDtypeStruct((units, features), BF16)],
        aliases={3 + given: 0} if extra else {},
        scratch=slots.scratch()
        + [
            pltpu.VMEM((ahead, tile, rows_all), BF16),
            pltpu.VMEM((behind, count, tile, part), BF16),
            pltpu.SemaphoreType.DMA((ahead,)),
            pltpu.SemaphoreType.DMA((behind, count)),
        ],
        flops=2 * rows_all * units * part * count,
        size=2 * units * part * count,
    )


def tie(values, *deps):
    count = len(values)

    def body(*refs):
        pass

    return pl.pallas_call(
        body,
        in_specs=[ANY] * (count + len(deps)),
        out_specs=[ANY] * count,
        out_shape=[jax.ShapeDtypeStruct(v.shape, v.dtype) for v in values],
        input_output_aliases={i: i for i in range(count)},
        compiler_params=params(),
    )(*values, *deps)


def choose(flags, pairs, values, deps):
    arrays = [piece for pair in pairs for block in pair for piece in block]
    tokens, part = sum(p.shape[0] for p in pairs[0][0]), pairs[0][0][0].shape[1]
    count, kept = len(arrays), len(values)

    def body(f_ref, *refs):
        o_ref, semaphore = refs[-2 - kept], refs[-1]
        given = iter(refs[:count])
        for j, pair in enumerate(pairs):
            for wanted, block in zip((1, 0), pair):
                copies, row = [], j * tokens
                for piece in block:
                    size = piece.shape[0]
                    copies.append(pltpu.make_async_copy(next(given), o_ref.at[pl.ds(row, size)], semaphore))
                    row += size

                @pl.when(f_ref[j] == wanted)
                def _(copies=copies):
                    for copy in copies:
                        copy.start()

        pltpu.make_async_copy(o_ref, o_ref, semaphore).wait()

    return pl.pallas_call(
        body,
        in_specs=[pl.BlockSpec(memory_space=pltpu.SMEM)] + [ANY] * (count + kept + len(deps)),
        out_specs=[ANY] * (1 + kept),
        out_shape=[jax.ShapeDtypeStruct((len(pairs) * tokens, part), BF16)]
        + [jax.ShapeDtypeStruct(v.shape, v.dtype) for v in values],
        input_output_aliases={1 + count + i: 1 + i for i in range(kept)},
        scratch_shapes=[pltpu.SemaphoreType.DMA],
        compiler_params=params(),
    )(flags, *arrays, *values, *deps)


def ring_shards(n, gate_input, up_input, code_values, exponents, cotangent):
    tokens, part = cotangent.shape
    units, features = code_values.shape
    lines = n // 2
    ring = [2 * p for p in range(lines)] + [2 * (n - 1 - p) + 1 for p in range(lines, n)]
    forward = [(ring[p], ring[(p + 1) % n]) for p in range(n)]
    backward = [(b, a) for a, b in forward]
    core = lax.axis_index("depth")
    index = lax.axis_index("grid")
    line = index // 2
    here = jnp.where(index % 2 == 0, line, n - 1 - line)

    def owner(offset):
        p = (here + offset + n) % n
        return jnp.where(p < lines, 2 * p, 2 * (n - 1 - p) + 1)

    def swap(value):
        return lax.ppermute(value, "depth", SWAP)

    def on(value):
        return lax.ppermute(value, "grid", forward)

    def back(value):
        return lax.ppermute(value, "grid", backward)

    pairs = [(4, 0), (3, -1), (-3, 1), (2, -2)]
    mine = [owner(a) // lines == core for a, _ in pairs]
    place = [jnp.where(m, owner(a), owner(b)) % lines for (a, b), m in zip(pairs, mine)]

    def places(*group):
        return jnp.stack([place[j] for j in group]).astype(jnp.int32)

    def flags(*group):
        return jnp.stack([mine[j] for j in group]).astype(jnp.int32)

    half = tokens // 2
    block, got, term = {0: [cotangent]}, {}, {}

    def pieces(rows):
        return [(piece, 0, piece.shape[0]) for piece in rows]

    def terms(*group, deps=()):
        own, others, *turned = output_terms(
            places(*group), hidden, hidden_other, code_values, exponents, part, deps, group == (0,)
        )
        return own, swap(others), *turned

    def keep_terms(group, own, others):
        for i, j in enumerate(group):
            a, b = pairs[j]
            here, there = (rows[i * tokens : (i + 1) * tokens] for rows in (own, others))
            term[a] = jnp.where(mine[j], here, there)
            term[b] = jnp.where(mine[j], there, here)

    def slots(*group):
        return Slots([[pieces(block[a]), pieces(block[b]), got[j]] for j in group for a, b in (pairs[j],)])

    def weight_phase(so_far, group):
        return weight_gradient(places(*group), flags(*group), slots(*group), turned, so_far, features)

    def gradient(so_far, group, deps=()):
        (((out,)),) = run([weight_phase(so_far, group)], deps)
        return out

    def add(value, other):
        return (value.astype(F32) + other.astype(F32)).astype(BF16)

    def exchange(group, values, *deps):
        chosen = [(block[pairs[j][1]], block[pairs[j][0]]) for j in group]
        given, *values = choose(flags(*group), chosen, values, deps)
        found = swap(given)
        for i, j in enumerate(group):
            got[j] = [(found, i * tokens, tokens)]
        return values

    block[-1], block[1] = [on(cotangent)], [back(cotangent)]
    hidden = make_hidden(gate_input, up_input)
    hidden_other = swap(hidden)

    own_a, others_a, turned = terms(0)
    first, second = tie([block[-1][0], block[1][0]], own_a)
    block[-1], block[1] = [first], [second]
    block[-2], block[2] = [on(first)], [back(second)]

    own_b, others_b = terms(1, 2, deps=(first, second))
    first, second = tie([block[-2][0], block[2][0]], own_b)
    block[-2], block[2] = [first], [second]
    block[-3], block[3] = [on(first)], [back(second)]
    exchange((3,), [])

    own_c, others_c = terms(3, deps=(first, second))
    (others_a,) = tie([others_a], own_c)
    keep_terms((0,), own_a, others_a)
    up, down = on(term[4][:half]), back(term[4][half:])
    grad_weight = gradient(None, (3,), (own_c, term[4]))

    first, second, up, down = tie([block[-3][0], block[3][0], up, down], grad_weight)
    block[-3], block[3] = [first], [second]
    block[4] = [on(first[:half]), back(second[half:])]
    exchange((1, 2), [])
    keep_terms((1, 2), own_b, others_b)
    zero = jnp.zeros((half, part), BF16)
    up, down = add(jnp.concatenate([up, zero], 0), term[3]), add(jnp.concatenate([zero, down], 0), term[-3])
    deps = (up, down)
    up, down = on(up), back(down)
    grad_weight = gradient(grad_weight, (1, 2), deps)

    *block[4], up, down = tie([*block[4], up, down], grad_weight)
    exchange((0,), [])
    keep_terms((3,), own_c, others_c)
    up, down = add(up, term[2]), add(down, term[-2])
    deps = (up, down)
    up, down = on(up), back(down)

    everything = slots(0, 1, 2, 3)
    width = units // 2

    def hidden_phase(start, alone):
        return hidden_gradient(
            places(0, 1, 2, 3), flags(0, 1, 2, 3), everything, code_values, exponents, start, width, alone
        )

    (grad_weight,), (own_left, give) = run([weight_phase(grad_weight, (0,)), hidden_phase(0, False)], deps, 36 * 1024 * 1024)
    other_left = swap(give)
    up, down = tie([up, down], give)
    up, down = add(up, term[1]), add(down, term[-1])
    deps = (up, down)
    up, down = on(up), back(down)
    ((own_right, give),) = run([hidden_phase(width, True)], deps)
    other_right = swap(give)
    done = finish(gate_input, up_input, own_left, other_left, 0, [], give)
    output_rows = (up.astype(F32) + down.astype(F32) + term[0].astype(F32)).astype(BF16)
    done = finish(gate_input, up_input, own_right, other_right, width, done, output_rows)
    return output_rows, done[0], done[1], grad_weight


def any_shards(n, gate_input, up_input, code_values, exponents, cotangent):
    tokens, part = cotangent.shape
    units, features = code_values.shape
    core = lax.axis_index("depth")
    half = n // 2
    gathered = lax.all_gather(cotangent, "grid", axis=0, tiled=False)
    hidden = make_hidden(gate_input, up_input)
    hidden_other = lax.ppermute(hidden, "depth", SWAP)
    place, flag = jnp.zeros((1,), jnp.int32), jnp.ones((1,), jnp.int32)

    own, other, turned = output_terms(
        place, hidden, hidden_other, code_values, exponents, features, turn=True
    )
    got = lax.ppermute(other, "depth", SWAP)
    first = jnp.where(core == 0, own, got).reshape(tokens, half, part)
    second = jnp.where(core == 0, got, own).reshape(tokens, half, part)
    pieces = jnp.concatenate([first, second], 1).transpose(1, 0, 2)
    output_rows = lax.psum_scatter(pieces, "grid", scatter_dimension=0, tiled=False)

    keep = lax.dynamic_slice_in_dim(gathered, core * half, half, 0)
    give = lax.dynamic_slice_in_dim(gathered, (1 - core) * half, half, 0)
    both = [keep, lax.ppermute(give, "depth", SWAP)]
    own, other = ([(v.transpose(1, 0, 2).reshape(tokens, features), 0, tokens)] for v in both)
    slots = Slots([[own, own, other]])
    ((grad_mine, grad_give),) = run([hidden_gradient(place, flag, slots, code_values, exponents, 0, units)])
    grad_other = lax.ppermute(grad_give, "depth", SWAP)
    ((grad_weight,),) = run([weight_gradient(place, flag, slots, turned, None, features)])
    grad_gate, grad_up = finish(gate_input, up_input, grad_mine, grad_other, 0, [])
    return output_rows, grad_gate, grad_up, grad_weight


def solution(mesh):
    n = mesh.shape["grid"]
    in_specs = (
        P(("parts", "depth"), "grid"),
        P(("parts", "depth"), "grid"),
        P("grid", "depth"),
        P("grid", "depth"),
        P(("parts", "depth"), "grid"),
    )
    out_specs = (
        P(("parts", "depth"), "grid"),
        P(("parts", "depth"), "grid"),
        P(("parts", "depth"), "grid"),
        P(("parts", "grid"), "depth"),
    )
    step = functools.partial(ring_shards if n == 8 else any_shards, n)
    return jax.shard_map(step, mesh=mesh, in_specs=in_specs, out_specs=out_specs, check_vma=False)
```

```python
import functools

import jax
import jax.numpy as jnp
from jax import lax
from jax.experimental import pallas as pl
from jax.experimental.pallas import tpu as pltpu
from jax.sharding import PartitionSpec as P

F32 = jnp.float32
BF16 = jnp.bfloat16
VMEM_BYTES = 30 * 1024 * 1024
SWAP = [(0, 1), (1, 0)]
ANY = pl.BlockSpec(memory_space=pl.ANY)


def params(size=VMEM_BYTES):
    return pltpu.CompilerParams(vmem_limit_bytes=size)


def cost(flops, size):
    return pl.CostEstimate(flops=flops, bytes_accessed=size, transcendentals=0)


def dequantize(codes, exponents):
    rows, columns = codes.shape
    scale = jnp.exp2(exponents.astype(F32)).astype(BF16)
    blocks = codes.reshape(rows // 32, 32, columns) * scale.reshape(rows // 32, 1, columns)
    return blocks.reshape(rows, columns)


def sigmoid(value):
    return 0.5 * jnp.tanh(0.5 * value) + 0.5


def make_hidden(gate, up):
    tokens, units = gate.shape
    tile = min(units, 1024)
    tiles = units // tile

    def body(g_ref, u_ref, h_ref, gate_held, up_held, out_held, in_sem, out_sem):
        def columns(i):
            return pl.ds(i * tile, tile)

        def store(i):
            return pltpu.make_async_copy(out_held.at[i], h_ref.at[:, columns(i)], out_sem.at[i])

        for i in range(tiles):
            pltpu.make_async_copy(g_ref.at[:, columns(i)], gate_held.at[i], in_sem.at[i, 0]).start()
            pltpu.make_async_copy(u_ref.at[:, columns(i)], up_held.at[i], in_sem.at[i, 1]).start()
        for i in range(tiles):
            wait(gate_held.at[i], in_sem.at[i, 0])
            wait(up_held.at[i], in_sem.at[i, 1])
            value = gate_held[i].astype(F32)
            out_held[i] = (value * sigmoid(value) * up_held[i].astype(F32)).astype(BF16)
            store(i).start()
        for i in range(tiles):
            store(i).wait()

    held = pltpu.VMEM((tiles, tokens, tile), BF16)
    return pl.pallas_call(
        body,
        in_specs=[ANY] * 2,
        out_specs=ANY,
        out_shape=jax.ShapeDtypeStruct((tokens, units), BF16),
        scratch_shapes=[held, held, held, pltpu.SemaphoreType.DMA((tiles, 2)), pltpu.SemaphoreType.DMA((tiles,))],
        compiler_params=params(60 * 1024 * 1024),
        cost_estimate=cost(10 * tokens * units, 6 * tokens * units),
    )(gate, up)


def finish(gate, up, mine, other, first, so_far, *deps):
    tokens, units = gate.shape
    width = mine.shape[1]
    tile = min(width, 1024)
    base = first // tile

    def body(g_ref, u_ref, m_ref, o_ref, *refs):
        dg_ref, du_ref = refs[-2:]
        value = g_ref[...].astype(F32)
        s = sigmoid(value)
        grad = m_ref[...].astype(F32) + o_ref[...].astype(F32)
        slope = s * (1.0 + value * (1.0 - s))
        dg_ref[...] = (grad * u_ref[...].astype(F32) * slope).astype(BF16)
        du_ref[...] = (grad * (value * s)).astype(BF16)

    there = pl.BlockSpec((tokens, tile), lambda i: (0, base + i))
    here = pl.BlockSpec((tokens, tile), lambda i: (0, i))
    shape = jax.ShapeDtypeStruct((tokens, units), BF16)
    return pl.pallas_call(
        body,
        grid=(width // tile,),
        in_specs=[there, there, here, here] + [ANY] * (len(so_far) + len(deps)),
        out_specs=[there] * 2,
        out_shape=[shape] * 2,
        input_output_aliases={4: 0, 5: 1} if so_far else {},
        compiler_params=params(),
        cost_estimate=cost(20000 * tokens * width, 1000 * tokens * width),
    )(gate, up, mine, other, *so_far, *deps)


def block(i, size):
    return pl.ds(pl.multiple_of(i * size, size), size)


def wait(ref, semaphore):
    pltpu.make_async_copy(ref, ref, semaphore).wait()


def output_terms(places, hidden, hidden_other, codes, exponents, part, deps=(), turn=False):
    tokens, units = hidden.shape
    tile = min(part, 512)
    step = min(units, 1024)
    count = places.shape[0]
    tiles = part // tile
    last = count * tiles
    steps = range(0, units, step)
    outputs = 3 if turn else 2

    def body(p_ref, h_ref, x_ref, c_ref, e_ref, *refs):
        out = refs[len(deps) : len(deps) + outputs]
        held, codes_held, exponents_held, out_held, h_sem, c_sem, e_sem, o_sem, *more = refs[len(deps) + outputs :]

        def columns(i):
            return block(p_ref[i // tiles] * tiles + i % tiles, tile)

        def fetch(i, rows, semaphore):
            pltpu.make_async_copy(c_ref.at[rows, columns(i)], codes_held.at[i % 2, rows], semaphore).start()

        def fetch_exponents(i):
            pltpu.make_async_copy(e_ref.at[:, columns(i)], exponents_held.at[i % 2], e_sem.at[i % 2]).start()

        def stores(i):
            rows, lanes = block(i // tiles, tokens), block(i % tiles, tile)
            return [
                pltpu.make_async_copy(out_held.at[i % 2, :tokens], out[0].at[rows, lanes], o_sem.at[i % 2, 0]),
                pltpu.make_async_copy(out_held.at[i % 2, tokens:], out[1].at[rows, lanes], o_sem.at[i % 2, 1]),
            ]

        fetch_exponents(0)
        for n, k in enumerate(steps):
            rows = pl.ds(k, step)
            pltpu.make_async_copy(h_ref.at[:, rows], held.at[:tokens, rows], h_sem.at[n]).start()
            pltpu.make_async_copy(x_ref.at[:, rows], held.at[tokens:, rows], h_sem.at[n]).start()
            fetch(0, rows, c_sem.at[n])
        if last > 1:
            fetch_exponents(1)
            fetch(1, pl.ds(0, units), c_sem.at[len(steps)])

        def work(i):
            wait(exponents_held.at[i % 2], e_sem.at[i % 2])
            total = None
            for n, k in enumerate(steps):
                rows = pl.ds(k, step)
                if isinstance(i, int):
                    wait(held.at[:, rows], h_sem.at[n])
                    wait(codes_held.at[0, rows], c_sem.at[n])
                weight = dequantize(codes_held[i % 2, rows], exponents_held[i % 2, k // 32 : (k + step) // 32, :])
                term = jnp.dot(held[:, rows], weight, preferred_element_type=F32)
                total = term if total is None else total + term
                if turn and isinstance(i, int):
                    turned_held, t_sem = more
                    turned_held[rows] = held[:, rows].T
                    pltpu.make_async_copy(turned_held.at[rows], out[2].at[rows], t_sem.at[n]).start()
            return total.astype(BF16)

        def go_on(i):
            for copy in stores(i):
                copy.start()

            @pl.when(i + 2 < last)
            def _():
                fetch_exponents(i + 2)
                fetch(i + 2, pl.ds(0, units), c_sem.at[len(steps) + (i + 1) % 2])

        out_held[0] = work(0)
        go_on(0)

        @pl.loop(1, last)
        def _(i):
            wait(codes_held.at[i % 2], c_sem.at[len(steps) + (i + 1) % 2])
            total = work(i)

            @pl.when(i >= 2)
            def _():
                for copy in stores(i - 2):
                    copy.wait()

            out_held[i % 2] = total
            go_on(i)

        for i in range(max(0, last - 2), last):
            for copy in stores(i):
                copy.wait()
        if turn:
            turned_held, t_sem = more
            for n, k in enumerate(steps):
                wait(turned_held.at[pl.ds(k, step)], t_sem.at[n])

    out = pl.pallas_call(
        body,
        in_specs=[pl.BlockSpec(memory_space=pltpu.SMEM)] + [ANY] * (4 + len(deps)),
        out_specs=[ANY] * outputs,
        out_shape=[jax.ShapeDtypeStruct((count * tokens, part), BF16)] * 2
        + ([jax.ShapeDtypeStruct((units, 2 * tokens), BF16)] if turn else []),
        scratch_shapes=[
            pltpu.VMEM((2 * tokens, units), BF16),
            pltpu.VMEM((2, units, tile), BF16),
            pltpu.VMEM((2, units // 32, tile), jnp.int32),
            pltpu.VMEM((2, 2 * tokens, tile), BF16),
            pltpu.SemaphoreType.DMA((len(steps),)),
            pltpu.SemaphoreType.DMA((len(steps) + 2,)),
            pltpu.SemaphoreType.DMA((2,)),
            pltpu.SemaphoreType.DMA((2, 2)),
        ]
        + ([pltpu.VMEM((units, 2 * tokens), BF16), pltpu.SemaphoreType.DMA((len(steps),))] if turn else []),
        compiler_params=params(),
        cost_estimate=cost(4 * tokens * units * part * count, 2 * units * part * count),
    )(places, hidden, hidden_other, codes, exponents, *deps)
    return out


class Slots:
    def __init__(self, blocks):
        self.blocks = blocks
        self.arrays = [piece[0] for block in blocks for rows in block for piece in rows]
        self.tokens = sum(piece[2] for piece in blocks[0][2])
        self.part = blocks[0][2][0][0].shape[1]

    def scratch(self):
        return [
            pltpu.VMEM((len(self.blocks), 2 * self.tokens, self.part), BF16),
            pltpu.SemaphoreType.DMA((len(self.blocks),)),
        ]

    def load(self, j, flags, refs, held, semaphores):
        before = sum(len(rows) for block in self.blocks[:j] for rows in block)
        refs = iter(refs[before:])
        for wanted, rows in zip((1, 0, None), self.blocks[j]):
            copies, row = [], self.tokens if wanted is None else 0
            for _, first, size in rows:
                copies.append(
                    pltpu.make_async_copy(
                        next(refs).at[pl.ds(first, size)], held.at[j, pl.ds(row, size)], semaphores.at[j]
                    )
                )
                row += size

            def start(copies=copies):
                for copy in copies:
                    copy.start()

            if wanted is None:
                start()
            else:
                pl.when(flags[j] == wanted)(start)


def run(phases, deps=(), size=VMEM_BYTES):
    smem = pl.BlockSpec(memory_space=pltpu.SMEM)
    ends = []
    aliases = {}
    given, made, held = 0, 0, 0
    for phase in phases:
        for i, o in phase["aliases"].items():
            aliases[given + i] = made + o
        ends.append((given, made, held))
        given += phase["scalars"] + len(phase["inputs"])
        made += len(phase["shapes"])
        held += len(phase["scratch"])
    ends.append((given, made, held))

    def body(*refs):
        inputs, outputs = refs[:given], refs[given + len(deps) : given + len(deps) + made]
        scratch = refs[given + len(deps) + made :]
        steps = []
        for phase, (i, o, h), (i_end, o_end, h_end) in zip(phases, ends, ends[1:]):
            steps.append(phase["body"](*inputs[i:i_end], *outputs[o:o_end], *scratch[h:h_end]))
        for step in steps:
            next(step)
        for step in steps:
            next(step, None)

    out = pl.pallas_call(
        body,
        in_specs=[
            spec for p in phases for spec in [smem] * p["scalars"] + [ANY] * len(p["inputs"])
        ]
        + [ANY] * len(deps),
        out_specs=[ANY] * made,
        out_shape=[shape for p in phases for shape in p["shapes"]],
        input_output_aliases=aliases,
        scratch_shapes=[shape for p in phases for shape in p["scratch"]],
        compiler_params=params(size),
        cost_estimate=cost(sum(p["flops"] for p in phases), sum(p["size"] for p in phases)),
    )(*[value for p in phases for value in p["numbers"] + p["inputs"]], *deps)
    return [out[a[1] : b[1]] for a, b in zip(ends, ends[1:])]


def hidden_gradient(places, flags, slots, codes, exponents, first, width, alone=True):
    tokens, part, count = slots.tokens, slots.part, len(slots.blocks)
    tile = min(width, 512)
    tiles = width // tile
    given = len(slots.arrays)
    step = min(part, 1024)

    def body(p_ref, f_ref, *refs):
        c_ref, e_ref = refs[given : given + 2]
        m_ref, o_ref, held, t_sem, codes_held, exponents_held, m_held, o_held, c_sem, e_sem, o_sem = refs[given + 2 :]

        def columns(j):
            return pl.ds(pl.multiple_of(p_ref[j] * part, part), part)

        def fetch(i, j):
            rows = pl.ds(first + pl.multiple_of(i * tile, tile), tile)
            pltpu.make_async_copy(c_ref.at[rows, columns(j)], codes_held.at[i % 2, j], c_sem.at[i % 2, j]).start()

        def stores(i):
            lanes = block(i, tile)
            return [
                pltpu.make_async_copy(m_held.at[i % 2], m_ref.at[:, lanes], o_sem.at[i % 2, 0]),
                pltpu.make_async_copy(o_held.at[i % 2], o_ref.at[:, lanes], o_sem.at[i % 2, 1]),
            ]

        for j in range(count):
            slots.load(j, f_ref, refs[:given], held, t_sem)
            fetch(0, j)
            rows = pl.ds(first // 32, width // 32)
            pltpu.make_async_copy(e_ref.at[rows, columns(j)], exponents_held.at[j], e_sem.at[j]).start()
        if tiles > 1:
            for j in range(count):
                fetch(1, j)
        yield

        def arrive(j):
            wait(held.at[j], t_sem.at[j])
            wait(exponents_held.at[j], e_sem.at[j])

        def work(i, step_by_step):
            if not step_by_step:
                for j in range(count):
                    wait(codes_held.at[i % 2, j], c_sem.at[i % 2, j])
            total = None
            for j in range(count):
                if step_by_step:
                    arrive(j)
                    wait(codes_held.at[i % 2, j], c_sem.at[i % 2, j])
                for k in range(0, part, step):
                    lanes = pl.ds(k, step)
                    weight = dequantize(
                        codes_held[i % 2, j, :, lanes], exponents_held[j, block(i, tile // 32), lanes]
                    )
                    term = lax.dot_general(
                        held[j, :, lanes], weight, (((1,), (1,)), ((), ())), preferred_element_type=F32
                    )
                    total = term if total is None else total + term

            @pl.when(i >= 2)
            def _():
                for copy in stores(i - 2):
                    copy.wait()

            m_held[i % 2] = total[:tokens].astype(BF16)
            o_held[i % 2] = total[tokens:].astype(BF16)
            for copy in stores(i):
                copy.start()

            @pl.when(i + 2 < tiles)
            def _():
                for j in range(count):
                    fetch(i + 2, j)

        if alone:
            work(0, True)
        else:
            for j in range(count):
                arrive(j)

        @pl.loop(1 if alone else 0, tiles)
        def _(i):
            work(i, False)

        for i in range(max(0, tiles - 2), tiles):
            for copy in stores(i):
                copy.wait()

    return dict(
        body=body,
        scalars=2,
        numbers=[places, flags],
        inputs=[*slots.arrays, codes, exponents],
        shapes=[jax.ShapeDtypeStruct((tokens, width), BF16)] * 2,
        aliases={},
        scratch=slots.scratch()
        + [
            pltpu.VMEM((2, count, tile, part), BF16),
            pltpu.VMEM((count, width // 32, part), jnp.int32),
            pltpu.VMEM((2, tokens, tile), BF16),
            pltpu.VMEM((2, tokens, tile), BF16),
            pltpu.SemaphoreType.DMA((2, count)),
            pltpu.SemaphoreType.DMA((count,)),
            pltpu.SemaphoreType.DMA((2, 2)),
        ],
        flops=4 * tokens * width * part * count,
        size=2 * width * part * count,
    )


def weight_gradient(places, flags, slots, turned, so_far, features):
    part, count = slots.part, len(slots.blocks)
    units, rows_all = turned.shape
    tile = min(units, 512)
    tiles = units // tile
    given = len(slots.arrays)
    step = min(part, 1024)
    ahead = min(4, tiles)
    behind = min(4, tiles)

    def body(p_ref, f_ref, *refs):
        h_ref = refs[given]
        w_ref, held, t_sem, turned_held, out_held, h_sem, o_sem = refs[-7:]

        def fetch(i):
            slot = i % ahead
            pltpu.make_async_copy(h_ref.at[block(i, tile)], turned_held.at[slot], h_sem.at[slot]).start()

        def store(i, j):
            columns = pl.ds(pl.multiple_of(p_ref[j] * part, part), part)
            return pltpu.make_async_copy(
                out_held.at[i % behind, j], w_ref.at[block(i, tile), columns], o_sem.at[i % behind, j]
            )

        fetch(0)
        for j in range(count):
            slots.load(j, f_ref, refs[:given], held, t_sem)
        for i in range(1, ahead):
            fetch(i)
        yield

        @pl.loop(0, tiles)
        def _(i):
            wait(turned_held.at[i % ahead], h_sem.at[i % ahead])
            left = turned_held[i % ahead]

            @pl.when(i >= behind)
            def _():
                for j in range(count):
                    store(i - behind, j).wait()

            for j in range(count):

                @pl.when(i == 0)
                def _(j=j):
                    wait(held.at[j], t_sem.at[j])

                for k in range(0, part, step):
                    lanes = pl.ds(k, step)
                    out_held[i % behind, j, :, lanes] = jnp.dot(
                        left, held[j, :, lanes], preferred_element_type=F32
                    ).astype(BF16)
                store(i, j).start()

            @pl.when(i + ahead < tiles)
            def _():
                fetch(i + ahead)

        for i in range(tiles - behind, tiles):
            for j in range(count):
                store(i, j).wait()

    extra = [] if so_far is None else [so_far]
    return dict(
        body=body,
        scalars=2,
        numbers=[places, flags],
        inputs=[*slots.arrays, turned, *extra],
        shapes=[jax.ShapeDtypeStruct((units, features), BF16)],
        aliases={3 + given: 0} if extra else {},
        scratch=slots.scratch()
        + [
            pltpu.VMEM((ahead, tile, rows_all), BF16),
            pltpu.VMEM((behind, count, tile, part), BF16),
            pltpu.SemaphoreType.DMA((ahead,)),
            pltpu.SemaphoreType.DMA((behind, count)),
        ],
        flops=2 * rows_all * units * part * count,
        size=2 * units * part * count,
    )


def tie(values, *deps):
    count = len(values)

    def body(*refs):
        pass

    return pl.pallas_call(
        body,
        in_specs=[ANY] * (count + len(deps)),
        out_specs=[ANY] * count,
        out_shape=[jax.ShapeDtypeStruct(v.shape, v.dtype) for v in values],
        input_output_aliases={i: i for i in range(count)},
        compiler_params=params(),
    )(*values, *deps)


def choose(flags, pairs, values, deps):
    arrays = [piece for pair in pairs for block in pair for piece in block]
    tokens, part = sum(p.shape[0] for p in pairs[0][0]), pairs[0][0][0].shape[1]
    count, kept = len(arrays), len(values)

    def body(f_ref, *refs):
        o_ref, semaphore = refs[-2 - kept], refs[-1]
        given = iter(refs[:count])
        for j, pair in enumerate(pairs):
            for wanted, block in zip((1, 0), pair):
                copies, row = [], j * tokens
                for piece in block:
                    size = piece.shape[0]
                    copies.append(pltpu.make_async_copy(next(given), o_ref.at[pl.ds(row, size)], semaphore))
                    row += size

                @pl.when(f_ref[j] == wanted)
                def _(copies=copies):
                    for copy in copies:
                        copy.start()

        pltpu.make_async_copy(o_ref, o_ref, semaphore).wait()

    return pl.pallas_call(
        body,
        in_specs=[pl.BlockSpec(memory_space=pltpu.SMEM)] + [ANY] * (count + kept + len(deps)),
        out_specs=[ANY] * (1 + kept),
        out_shape=[jax.ShapeDtypeStruct((len(pairs) * tokens, part), BF16)]
        + [jax.ShapeDtypeStruct(v.shape, v.dtype) for v in values],
        input_output_aliases={1 + count + i: 1 + i for i in range(kept)},
        scratch_shapes=[pltpu.SemaphoreType.DMA],
        compiler_params=params(),
    )(flags, *arrays, *values, *deps)


def ring_shards(n, gate_input, up_input, code_values, exponents, cotangent):
    tokens, part = cotangent.shape
    units, features = code_values.shape
    lines = n // 2
    ring = [2 * p for p in range(lines)] + [2 * (n - 1 - p) + 1 for p in range(lines, n)]
    forward = [(ring[p], ring[(p + 1) % n]) for p in range(n)]
    backward = [(b, a) for a, b in forward]
    core = lax.axis_index("depth")
    index = lax.axis_index("grid")
    line = index // 2
    here = jnp.where(index % 2 == 0, line, n - 1 - line)

    def owner(offset):
        p = (here + offset + n) % n
        return jnp.where(p < lines, 2 * p, 2 * (n - 1 - p) + 1)

    def swap(value):
        return lax.ppermute(value, "depth", SWAP)

    def on(value):
        return lax.ppermute(value, "grid", forward)

    def back(value):
        return lax.ppermute(value, "grid", backward)

    pairs = [(4, 0), (3, -1), (-3, 1), (2, -2)]
    mine = [owner(a) // lines == core for a, _ in pairs]
    place = [jnp.where(m, owner(a), owner(b)) % lines for (a, b), m in zip(pairs, mine)]

    def places(*group):
        return jnp.stack([place[j] for j in group]).astype(jnp.int32)

    def flags(*group):
        return jnp.stack([mine[j] for j in group]).astype(jnp.int32)

    half = tokens // 2
    block, got, term = {0: [cotangent]}, {}, {}

    def pieces(rows):
        return [(piece, 0, piece.shape[0]) for piece in rows]

    def terms(*group, deps=()):
        own, others, *turned = output_terms(
            places(*group), hidden, hidden_other, code_values, exponents, part, deps, group == (0,)
        )
        return own, swap(others), *turned

    def keep_terms(group, own, others):
        for i, j in enumerate(group):
            a, b = pairs[j]
            here, there = (rows[i * tokens : (i + 1) * tokens] for rows in (own, others))
            term[a] = jnp.where(mine[j], here, there)
            term[b] = jnp.where(mine[j], there, here)

    def slots(*group):
        return Slots([[pieces(block[a]), pieces(block[b]), got[j]] for j in group for a, b in (pairs[j],)])

    def weight_phase(so_far, group):
        return weight_gradient(places(*group), flags(*group), slots(*group), turned, so_far, features)

    def gradient(so_far, group, deps=()):
        (((out,)),) = run([weight_phase(so_far, group)], deps)
        return out

    def add(value, other):
        return (value.astype(F32) + other.astype(F32)).astype(BF16)

    def exchange(group, values, *deps):
        chosen = [(block[pairs[j][1]], block[pairs[j][0]]) for j in group]
        given, *values = choose(flags(*group), chosen, values, deps)
        found = swap(given)
        for i, j in enumerate(group):
            got[j] = [(found, i * tokens, tokens)]
        return values

    block[-1], block[1] = [on(cotangent)], [back(cotangent)]
    hidden = make_hidden(gate_input, up_input)
    hidden_other = swap(hidden)

    own_a, others_a, turned = terms(0)
    first, second = tie([block[-1][0], block[1][0]], own_a)
    block[-1], block[1] = [first], [second]
    block[-2], block[2] = [on(first)], [back(second)]

    own_b, others_b = terms(1, 2, deps=(first, second))
    first, second = tie([block[-2][0], block[2][0]], own_b)
    block[-2], block[2] = [first], [second]
    block[-3], block[3] = [on(first)], [back(second)]
    exchange((3,), [])

    own_c, others_c = terms(3, deps=(first, second))
    (others_a,) = tie([others_a], own_c)
    keep_terms((0,), own_a, others_a)
    up, down = on(term[4][:half]), back(term[4][half:])
    grad_weight = gradient(None, (3,), (own_c, term[4]))

    first, second, up, down = tie([block[-3][0], block[3][0], up, down], grad_weight)
    block[-3], block[3] = [first], [second]
    block[4] = [on(first[:half]), back(second[half:])]
    exchange((1, 2), [])
    keep_terms((1, 2), own_b, others_b)
    zero = jnp.zeros((half, part), BF16)
    up, down = add(jnp.concatenate([up, zero], 0), term[3]), add(jnp.concatenate([zero, down], 0), term[-3])
    deps = (up, down)
    up, down = on(up), back(down)
    grad_weight = gradient(grad_weight, (1, 2), deps)

    *block[4], up, down = tie([*block[4], up, down], grad_weight)
    exchange((0,), [])
    keep_terms((3,), own_c, others_c)
    up, down = add(up, term[2]), add(down, term[-2])
    deps = (up, down)
    up, down = on(up), back(down)

    everything = slots(0, 1, 2, 3)
    width = units // 2

    def hidden_phase(start, alone):
        return hidden_gradient(
            places(0, 1, 2, 3), flags(0, 1, 2, 3), everything, code_values, exponents, start, width, alone
        )

    (grad_weight,), (own_left, give) = run([weight_phase(grad_weight, (0,)), hidden_phase(0, False)], deps, 36 * 1024 * 1024)
    other_left = swap(give)
    up, down = tie([up, down], give)
    up, down = add(up, term[1]), add(down, term[-1])
    deps = (up, down)
    up, down = on(up), back(down)
    ((own_right, give),) = run([hidden_phase(width, True)], deps)
    other_right = swap(give)
    done = finish(gate_input, up_input, own_left, other_left, 0, [], give)
    output_rows = (up.astype(F32) + down.astype(F32) + term[0].astype(F32)).astype(BF16)
    done = finish(gate_input, up_input, own_right, other_right, width, done, output_rows)
    return output_rows, done[0], done[1], grad_weight


def any_shards(n, gate_input, up_input, code_values, exponents, cotangent):
    tokens, part = cotangent.shape
    units, features = code_values.shape
    core = lax.axis_index("depth")
    half = n // 2
    gathered = lax.all_gather(cotangent, "grid", axis=0, tiled=False)
    hidden = make_hidden(gate_input, up_input)
    hidden_other = lax.ppermute(hidden, "depth", SWAP)
    place, flag = jnp.zeros((1,), jnp.int32), jnp.ones((1,), jnp.int32)

    own, other, turned = output_terms(
        place, hidden, hidden_other, code_values, exponents, features, turn=True
    )
    got = lax.ppermute(other, "depth", SWAP)
    first = jnp.where(core == 0, own, got).reshape(tokens, half, part)
    second = jnp.where(core == 0, got, own).reshape(tokens, half, part)
    pieces = jnp.concatenate([first, second], 1).transpose(1, 0, 2)
    output_rows = lax.psum_scatter(pieces, "grid", scatter_dimension=0, tiled=False)

    keep = lax.dynamic_slice_in_dim(gathered, core * half, half, 0)
    give = lax.dynamic_slice_in_dim(gathered, (1 - core) * half, half, 0)
    both = [keep, lax.ppermute(give, "depth", SWAP)]
    own, other = ([(v.transpose(1, 0, 2).reshape(tokens, features), 0, tokens)] for v in both)
    slots = Slots([[own, own, other]])
    ((grad_mine, grad_give),) = run([hidden_gradient(place, flag, slots, code_values, exponents, 0, units)])
    grad_other = lax.ppermute(grad_give, "depth", SWAP)
    ((grad_weight,),) = run([weight_gradient(place, flag, slots, turned, None, features)])
    grad_gate, grad_up = finish(gate_input, up_input, grad_mine, grad_other, 0, [])
    return output_rows, grad_gate, grad_up, grad_weight


def solution(mesh):
    n = mesh.shape["grid"]
    in_specs = (
        P(("parts", "depth"), "grid"),
        P(("parts", "depth"), "grid"),
        P("grid", "depth"),
        P("grid", "depth"),
        P(("parts", "depth"), "grid"),
    )
    out_specs = (
        P(("parts", "depth"), "grid"),
        P(("parts", "depth"), "grid"),
        P(("parts", "depth"), "grid"),
        P(("parts", "grid"), "depth"),
    )
    step = functools.partial(ring_shards if n == 8 else any_shards, n)
    return jax.shard_map(step, mesh=mesh, in_specs=in_specs, out_specs=out_specs, check_vma=False)
```
